32 devices in a mesh: grp: 4 (over x, core), ep: 8 (over z, y).
Axes of the slice: x: 2, y: 2, z: 4, core: 2. Of those that a mesh axis runs over, the one named last changes fastest.
Arguments:
- tokens: bfloat16 [1024, 3584], P('ep', 'grp'), may hold values from -6 to 6
- routes: int32 [1024, 1], P('ep'), may hold values from 0 to 7; in each aligned block of 128 rows (0 to 127, 128 to 255, ...) at most 32 rows name the same one
- route_weights: float32 [1024, 1], P('ep'), may hold values from 0.2 to 1
- hot_experts: int32 [4], replicated, may hold values from 0 to 3, as said below
- w_gate: bfloat16 [4, 3584, 2048], P(None, 'ep', 'grp'), may hold values from -0.09375 to 0.09375
- w_up: bfloat16 [4, 3584, 2048], P(None, 'ep', 'grp'), may hold values from -0.09375 to 0.09375
- w_down: bfloat16 [4, 2048, 3584], P(None, 'grp', 'ep'), may hold values from -0.125 to 0.125
- cotangent: bfloat16 [1024, 3584], P('ep', 'grp'), may hold values from -3 to 3
Outputs:
- layer_output: bfloat16 [1024, 3584], P('ep', 'grp')
- grad_tokens: bfloat16 [1024, 3584], P('ep', 'grp')
- grad_gate: bfloat16 [4, 3584, 2048], P(None, 'ep', 'grp')
- grad_up: bfloat16 [4, 3584, 2048], P(None, 'ep', 'grp')
- grad_down: bfloat16 [4, 2048, 3584], P(None, 'grp', 'ep')
The draws below stay inside these ranges and needn't reach their ends.
Inputs may be any that keep to these rules, and one draw needn't show every extreme that they name: `routes`: each row names one slot. Among the rows of one device (aligned blocks of 128 rows) no slot is named by more than 32 rows. `hot_experts`: entry j is the expert held by slot 4 + j; an expert may appear several times.
All inputs are finite; a program needn't handle non-finite values.
Results may differ from the reference program's by a relative error of at most 0.02.
Values may be sent and summed in bfloat16 or wider, within the bound.
No kernel may reach another device: no remote copies, remote signals or barrier semaphores. Data moves between devices by JAX's collectives and lax.ppermute only.
A program may use at most 128 MiB of HBM per device.

```python
import math
import jax
import jax.numpy as jnp
import numpy as np
from jax import lax

D = 3584
FF = 2048
TOP = 1
TOK_DEV = 128
TOKENS = 1024
EXPERTS = 4
REPLICAS = 4
CAP = 32
HID = 512
N_GRP = 4
N_EP = 8


def draw_hot_experts(key, part):
    values = jax.random.randint(key, (REPLICAS,), 0, EXPERTS, dtype=jnp.int32)
    values = values.at[0].set(EXPERTS - 1).at[1].set(0)
    return jax.random.permutation(jax.random.fold_in(key, 7), values)


def shard_levels(stream_key, shape, shards, low, high):
    level = 1.0
    for axis_at, blocks in shards:
        draws = jax.random.uniform(jax.random.fold_in(jax.random.fold_in(stream_key, 6), axis_at), (blocks,), jnp.float32, low / len(shards), high / len(shards))
        level = level * jnp.repeat(jnp.exp(draws), shape[axis_at] // blocks).reshape((-1,) + (1,) * (len(shape) - 1 - axis_at))
    return level


def shared_out(own_key, own, number, rows, number_of, top, limit, lean):
    ranking = jax.random.permutation(own_key, number_of)
    heavy_load, common = shares(number_of, rows * top, limit, lean, True), shares(number_of, rows * top, limit, lean, False)
    places = jnp.arange(number_of)

    def named(sizes, turn):
        used = int((sizes > 0).sum())
        fixed = max(1, used // 4)
        shifted = fixed + (places - fixed + turn * (used - fixed)) % max(1, number_of - fixed)
        return jnp.zeros((number_of,), jnp.int32).at[ranking[jnp.where(places < fixed, places, shifted)]].set(jnp.asarray(sizes, jnp.int32))

    sizes = jnp.where(number % 4 == 0, named(heavy_load, number // 4), named(common, number - number // 4 - 1))
    mixed = jax.random.permutation(jax.random.fold_in(own, 3), number_of)
    giver, sink = mixed[0:number_of // 2 * 2:2], mixed[1:number_of // 2 * 2:2]
    margin = jnp.minimum(sizes[giver] - 1, limit - sizes[sink]) // 2
    margin = jnp.where((giver == ranking[0]) | (sink == ranking[0]) | (sizes[sink] == 0), 0, jnp.maximum(margin, 0))
    shifted = jax.random.randint(jax.random.fold_in(own, 4), (number_of // 2,), 0, 1 << 20) % (margin + 1)
    sizes = sizes.at[giver].add(-shifted).at[sink].add(shifted)
    items = jnp.searchsorted(jnp.cumsum(sizes), jnp.arange(rows * top), side="right").astype(jnp.int32)
    table = items.reshape(top, rows).T
    table = table[jax.random.permutation(jax.random.fold_in(own, 1), rows)]
    turn = jax.random.randint(jax.random.fold_in(own, 2), (rows, 1), 0, top)
    return jnp.take_along_axis(table, (jnp.arange(top)[None, :] + turn) % top, axis=1)


def shares(amount, total, most, skew, full):
    portions = [(1 << 20) // math.isqrt(rank ** skew) + 1 for rank in range(1, amount + 1)]
    largest = most if full else min(most, max(-(-total // amount), total * portions[0] // sum(portions)))
    least = 1 if total - largest >= amount - 1 else 0
    holding, surplus = [largest] + [least] * (amount - 1), total - largest - least * (amount - 1)
    while surplus > 0:
        movable = [i for i in range(1, amount) if holding[i] < largest] or [i for i in range(1, amount) if holding[i] < most]
        whole, left = sum([portions[i] for i in movable]), surplus
        for i in movable:
            extra = min(most - holding[i], max(1, left * portions[i] // whole), surplus)
            holding[i] = holding[i] + extra
            surplus = surplus - extra
    return np.array(holding)


def scatter_about(stream_key, dims, scale, limit, split=(), held_as=jnp.bfloat16):
    factor_of = shard_levels(stream_key, dims, split, -0.22, 0.18) if split else 1.0
    result = jax.random.normal(stream_key, dims, jnp.float32) * scale * factor_of
    return jnp.minimum(jnp.maximum(result, -limit), limit).astype(held_as)


def setup_inputs(seed: int = 0) -> dict:
    streams_of = jax.random.split(jax.random.key(seed), 9)
    tokens = scatter_about(streams_of[0], (TOKENS, D), 1.0, 6.0, ((0, 8), (1, 4)))
    routes_keys = jax.random.split(jax.random.fold_in(streams_of[1], 1), TOKENS // TOK_DEV)
    routes_turns = jax.random.permutation(jax.random.fold_in(streams_of[1], 3), TOKENS // TOK_DEV)
    routes = jax.vmap(lambda own, number: shared_out(jax.random.fold_in(streams_of[1], 2), own, number, TOK_DEV, N_EP, TOP, CAP, 2))(routes_keys, routes_turns).reshape((TOKENS, TOP))
    route_weights = jnp.clip(0.2 + 0.8 * jax.random.uniform(streams_of[2], (TOKENS, TOP), jnp.float32) ** shard_levels(streams_of[2], (TOKENS, TOP), ((0, 8),), -0.2, 0.2), 0.2, 1.0)
    hot_experts = draw_hot_experts(jax.random.fold_in(streams_of[8], 71), 0)
    w_gate = scatter_about(streams_of[4], (EXPERTS, D, FF), D ** -0.5, 0.09375, ((1, 8), (2, 4)))
    w_up = scatter_about(streams_of[5], (EXPERTS, D, FF), D ** -0.5, 0.09375, ((1, 8), (2, 4)))
    w_down = scatter_about(streams_of[6], (EXPERTS, FF, D), FF ** -0.5, 0.125, ((1, 4), (2, 8)))
    cotangent = scatter_about(streams_of[7], (TOKENS, D), 0.5, 3.0, ((0, 8), (1, 4)))
    return dict(tokens=tokens, routes=routes, route_weights=route_weights, hot_experts=hot_experts, w_gate=w_gate, w_up=w_up, w_down=w_down, cotangent=cotangent)


def place_routes(slots_dev):
    onehot = (slots_dev[:, None] == jnp.arange(N_EP, dtype=jnp.int32)[None, :]).astype(jnp.int32)
    before = jnp.cumsum(onehot, axis=0) - onehot
    position = jnp.sum(before * onehot, axis=1).astype(jnp.int32)
    return (slots_dev * CAP + position).astype(jnp.int32)


def reference(tokens, routes, route_weights, hot_experts, w_gate, w_up, w_down, cotangent):
    flat_count = TOK_DEV * TOP
    pad_rows = N_EP * CAP
    slot_host = jnp.concatenate([jnp.arange(EXPERTS, dtype=jnp.int32), hot_experts.astype(jnp.int32)])
    dest = jax.vmap(place_routes)(routes.reshape(N_EP, flat_count).astype(jnp.int32))

    def source_of(target):
        base = jnp.full((pad_rows,), flat_count, jnp.int32)
        return base.at[target].set(jnp.arange(flat_count, dtype=jnp.int32))

    source = jax.vmap(source_of)(dest)
    dev_base = (jnp.arange(N_EP, dtype=jnp.int32) * flat_count)[:, None]
    global_src = jnp.where(source < flat_count, source + dev_base, TOKENS * TOP).astype(jnp.int32)
    global_src = global_src.reshape(N_EP, N_EP, CAP).transpose(1, 0, 2).reshape(N_EP, pad_rows)
    token_idx = (global_src // TOP).astype(jnp.int32)
    weight_ext = jnp.concatenate([route_weights.reshape(-1), jnp.zeros((1,), jnp.float32)])
    slot_weights = weight_ext[global_src]
    tokens_ext = jnp.concatenate([tokens, jnp.zeros((1, D), tokens.dtype)], axis=0)
    cot_ext = jnp.concatenate([cotangent, jnp.zeros((1, D), cotangent.dtype)], axis=0)

    def per_slot(carry, inputs):
        acc_gate, acc_up, acc_down = carry
        idx, wts, expert = inputs
        x_rows = tokens_ext[idx]
        dz_rows = (cot_ext[idx].astype(jnp.float32) * wts[:, None]).astype(jnp.bfloat16)
        wg = w_gate[expert]
        wu = w_up[expert]
        wd = w_down[expert]
        gate_pre = jnp.dot(x_rows, wg, preferred_element_type=jnp.float32)
        up_pre = jnp.dot(x_rows, wu, preferred_element_type=jnp.float32)
        sg = jax.nn.sigmoid(gate_pre)
        act = (gate_pre * sg * up_pre).astype(jnp.bfloat16)
        parts = jnp.einsum('rgh,ghd->rgd', act.reshape(pad_rows, N_GRP, HID).astype(jnp.float32),
                           wd.reshape(N_GRP, HID, D).astype(jnp.float32)).astype(jnp.bfloat16)
        out_sum = jnp.sum(parts.astype(jnp.float32), axis=1)
        act_grad = jnp.dot(dz_rows, wd.T, preferred_element_type=jnp.float32)
        gate_grad = (act_grad * up_pre * sg * (1.0 + gate_pre * (1.0 - sg))).astype(jnp.bfloat16)
        up_grad = (act_grad * gate_pre * sg).astype(jnp.bfloat16)
        tok_parts = jnp.einsum('rgh,dgh->rgd', gate_grad.reshape(pad_rows, N_GRP, HID).astype(jnp.float32),
                               wg.reshape(D, N_GRP, HID).astype(jnp.float32))
        tok_parts = tok_parts + jnp.einsum('rgh,dgh->rgd', up_grad.reshape(pad_rows, N_GRP, HID).astype(jnp.float32),
                                           wu.reshape(D, N_GRP, HID).astype(jnp.float32))
        tok_sum = jnp.sum(tok_parts.astype(jnp.bfloat16).astype(jnp.float32), axis=1)
        slot_gate = jnp.dot(x_rows.T, gate_grad, preferred_element_type=jnp.float32).astype(jnp.bfloat16)
        slot_up = jnp.dot(x_rows.T, up_grad, preferred_element_type=jnp.float32).astype(jnp.bfloat16)
        slot_down = jnp.dot(act.T, dz_rows, preferred_element_type=jnp.float32).astype(jnp.bfloat16)
        acc_gate = acc_gate.at[expert].add(slot_gate.astype(jnp.float32))
        acc_up = acc_up.at[expert].add(slot_up.astype(jnp.float32))
        acc_down = acc_down.at[expert].add(slot_down.astype(jnp.float32))
        return (acc_gate, acc_up, acc_down), (out_sum, tok_sum)

    init = (jnp.zeros((EXPERTS, D, FF), jnp.float32), jnp.zeros((EXPERTS, D, FF), jnp.float32),
            jnp.zeros((EXPERTS, FF, D), jnp.float32))
    (acc_gate, acc_up, acc_down), (out_all, tok_all) = lax.scan(per_slot, init, (token_idx, slot_weights, slot_host))
    slot_of = dest // CAP
    pos_of = dest % CAP
    flat_row = (slot_of * pad_rows + jnp.arange(N_EP, dtype=jnp.int32)[:, None] * CAP + pos_of).reshape(-1)
    out_routes = out_all.reshape(N_EP * pad_rows, D)[flat_row].reshape(TOKENS, TOP, D)
    tok_routes = tok_all.reshape(N_EP * pad_rows, D)[flat_row].reshape(TOKENS, TOP, D)
    layer_output = jnp.sum(route_weights[:, :, None] * out_routes, axis=1).astype(jnp.bfloat16)
    grad_tokens = jnp.sum(tok_routes, axis=1).astype(jnp.bfloat16)
    return (layer_output, grad_tokens, acc_gate.astype(jnp.bfloat16), acc_up.astype(jnp.bfloat16),
            acc_down.astype(jnp.bfloat16))
```

```python
import jax
import jax.numpy as jnp
from jax import lax
from jax.sharding import PartitionSpec as P

AXES = ("grp", "ep")


def swap(block, grp_bits, ep_bits):
    grp_size, ep_size = lax.axis_size("grp"), lax.axis_size("ep")
    pairs = [
        (g * ep_size + p, (g ^ grp_bits) * ep_size + (p ^ ep_bits))
        for g in range(grp_size)
        for p in range(ep_size)
    ]
    return lax.ppermute(block, AXES, pairs)


def to_plane(block, offset):
    grp_size, ep_size = lax.axis_size("grp"), lax.axis_size("ep")
    return [
        (g * ep_size + p, ((p // 2) ^ offset) * ep_size + 2 * g + p % 2)
        for g in range(grp_size)
        for p in range(ep_size)
    ]


def f32(a):
    return a.astype(jnp.float32)


def spread(rows):
    grp_size = lax.axis_size("grp")
    y = lax.axis_index("ep") % 2
    tok = rows.shape[0]
    half = rows.shape[1] // 2
    mine = lax.dynamic_slice_in_dim(rows, y * half, half, 1)
    other = lax.dynamic_slice_in_dim(rows, (1 - y) * half, half, 1)
    got = swap(other, 0, 1)
    per = grp_size // 2
    size = tok // per
    pieces = []
    for k in range(grp_size):
        source = mine if k < per else got
        piece = lax.slice_in_dim(source, (k % per) * size, (k % per + 1) * size, axis=0)
        pieces.append(lax.ppermute(piece, AXES, to_plane(piece, k)))
    held = jnp.stack(pieces)[None]
    order = [0]
    bit = grp_size // 2
    while bit:
        held = jnp.concatenate([held, swap(held, bit, 0)])
        order = order + [m ^ bit for m in order]
        bit //= 2
    return held, order


def unspread(parts, order):
    grp_size = lax.axis_size("grp")
    y = lax.axis_index("ep") % 2
    bit = 1
    held = parts
    while bit < grp_size:
        n = held.shape[0] // 2
        got = swap(held[n:], bit, 0)
        held = (f32(held[:n]) + f32(got)).astype(jnp.bfloat16)
        bit *= 2
    held = held[0]
    pieces = []
    for k in range(grp_size):
        back = [(b, a) for a, b in to_plane(None, k)]
        pieces.append(lax.ppermute(held[k], AXES, back))
    per = grp_size // 2
    mine = jnp.concatenate(pieces[:per])
    got = swap(jnp.concatenate(pieces[per:]), 0, 1)
    first = jnp.where(y == 0, mine, got)
    second = jnp.where(y == 0, got, mine)
    return jnp.concatenate([first, second], axis=1)


def scatter_sum(parts):
    got = swap(parts[1], 0, 1)
    zs = parts.shape[1]
    held = [(f32(parts[0, d]) + f32(got[d])) for d in range(zs)]
    total = held[0]
    for d in range(1, zs):
        total = total + f32(swap(held[d].astype(jnp.bfloat16), 0, 2 * d))
    return total


def gather(own):
    zs = lax.axis_size("ep") // 2
    line = jnp.stack([own] + [swap(own, 0, 2 * d) for d in range(1, zs)])
    return jnp.stack([line, swap(line, 0, 1)])


def shards(tokens, routes, route_weights, hot_experts, w_gate, w_up, w_down, cotangent):
    grp_size, ep_size = lax.axis_size("grp"), lax.axis_size("ep")
    zs = ep_size // 2
    g, p = lax.axis_index("grp"), lax.axis_index("ep")
    tok = tokens.shape[0]
    count, stored, hidden = w_gate.shape
    total = tok * ep_size
    slot_host = jnp.concatenate([jnp.arange(count, dtype=jnp.int32), hot_experts])
    slots = jnp.arange(slot_host.shape[0], dtype=jnp.int32)
    expert = jnp.sum(jnp.where(routes == slots[None, :], slot_host[None, :], 0), axis=1)
    experts = lax.all_gather(expert, "ep", axis=0)
    rel = jnp.arange(ep_size, dtype=jnp.int32).reshape(zs, 2).T.reshape(-1)
    expert_rel = jnp.take(experts, rel ^ p, axis=0).reshape(total)
    mask = expert_rel[:, None] == jnp.arange(count, dtype=jnp.int32)[None, :]

    def masked(rows):
        return jnp.where(mask[:, :, None], rows[:, None, :], jnp.zeros((), rows.dtype))

    per = grp_size // 2
    shift = g ^ (p // 2)

    def place_of(order):
        at = {m: i for i, m in enumerate(order)}
        return jnp.array([at[m] for m in range(grp_size)], jnp.int32)

    def to_relative(held, order):
        place = place_of(order)
        cols = []
        for k in range(grp_size):
            idx = place[shift ^ jnp.arange(zs, dtype=jnp.int32) ^ k]
            cols.append(jnp.take(held[:, k], idx, axis=0))
        both = [jnp.stack(cols[a * per : (a + 1) * per], axis=1) for a in range(2)]
        return jnp.stack(both).reshape(total, -1)

    def from_relative(rows, order):
        blocks = rows.reshape(2, zs, per, -1, rows.shape[-1])
        cols = []
        for k in range(grp_size):
            idx = shift ^ jnp.array(order, jnp.int32) ^ k
            cols.append(jnp.take(blocks[k // per, :, k % per], idx, axis=0))
        return jnp.stack(cols, axis=1)

    def dot(a, b, ca, cb):
        return lax.dot_general(a, b, ((ca, cb), ((), ())), preferred_element_type=jnp.float32)

    def half(a):
        return a.astype(jnp.bfloat16)

    x_held, order = spread(tokens)
    x_rows = to_relative(x_held, order)
    x_mask = masked(x_rows)

    def blocks(rows):
        return half(rows).reshape(2, zs, tok, -1)

    gate_pre = scatter_sum(blocks(dot(x_mask, w_gate, (1, 2), (0, 1))))
    up_pre = scatter_sum(blocks(dot(x_mask, w_up, (1, 2), (0, 1))))
    dz = half(f32(cotangent) * route_weights)
    dz_held, _ = spread(dz)
    dz_rows = to_relative(dz_held, order)
    dz_mask = masked(dz_rows)
    act_grad = scatter_sum(blocks(dot(dz_mask, w_down, (1, 2), (0, 2))))
    sg = jax.nn.sigmoid(gate_pre)
    act = half(gate_pre * sg * up_pre)
    gate_grad = half(act_grad * up_pre * sg * (1.0 + gate_pre * (1.0 - sg)))
    up_grad = half(act_grad * gate_pre * sg)
    act_rows = gather(act).reshape(total, hidden)
    act_mask = masked(act_rows)
    out_parts = half(dot(act_mask, w_down, (1, 2), (0, 1)))
    layer_output = half(f32(unspread(from_relative(out_parts, order), order)) * route_weights)
    gg_rows = gather(gate_grad).reshape(total, hidden)
    ug_rows = gather(up_grad).reshape(total, hidden)
    tok_parts = dot(masked(gg_rows), w_gate, (1, 2), (0, 2))
    tok_parts = half(tok_parts + dot(masked(ug_rows), w_up, (1, 2), (0, 2)))
    grad_tokens = unspread(from_relative(tok_parts, order), order)
    grad_down = half(dot(act_mask, dz_rows, (0,), (0,)))
    grad_gate = half(dot(x_mask, gg_rows, (0,), (0,)))
    grad_up = half(dot(x_mask, ug_rows, (0,), (0,)))
    return (layer_output, grad_tokens, grad_gate, grad_up, grad_down)


def solution(mesh):
    placed = (
        P("ep", "grp"),
        P("ep", None),
        P("ep", None),
        P(),
        P(None, "ep", "grp"),
        P(None, "ep", "grp"),
        P(None, "grp", "ep"),
        P("ep", "grp"),
    )
    return jax.shard_map(
        shards,
        mesh=mesh,
        in_specs=placed,
        out_specs=(
            P("ep", "grp"),
            P("ep", "grp"),
            P(None, "ep", "grp"),
            P(None, "ep", "grp"),
            P(None, "grp", "ep"),
        ),
        check_vma=False,
    )
```

```python
import functools

import jax
import jax.numpy as jnp
from jax import lax
from jax.experimental import pallas as pl
from jax.experimental.pallas import tpu as pltpu
from jax.sharding import PartitionSpec as P

AXES = ("grp", "ep")
BF16 = jnp.bfloat16
VMEM = pl.BlockSpec(memory_space=pltpu.VMEM)
SMEM = pl.BlockSpec(memory_space=pltpu.SMEM)
PARAMS = pltpu.CompilerParams(vmem_limit_bytes=50 * 1024 * 1024)


def f32(a):
    return a.astype(jnp.float32)


def half(a):
    return a.astype(BF16)


def swap(block, grp_bits, ep_bits):
    grp_size, ep_size = lax.axis_size("grp"), lax.axis_size("ep")
    pairs = [
        (g * ep_size + p, (g ^ grp_bits) * ep_size + (p ^ ep_bits))
        for g in range(grp_size)
        for p in range(ep_size)
    ]
    return lax.ppermute(block, AXES, pairs)


def plane_pairs(k):
    grp_size, ep_size = lax.axis_size("grp"), lax.axis_size("ep")
    flip = k // (grp_size // 2)
    return [
        (g * ep_size + p, ((p // 2) ^ k) * ep_size + 2 * g + ((p % 2) ^ flip))
        for g in range(grp_size)
        for p in range(ep_size)
    ]


def spread(mine, other):
    grp_size = lax.axis_size("grp")
    per = grp_size // 2
    size = mine.shape[0] // per
    pieces = []
    for k in range(grp_size):
        rows = (mine, other)[k // per][(k % per) * size : (k % per + 1) * size]
        pieces.append(lax.ppermute(rows, AXES, plane_pairs(k)))
    held = jnp.concatenate(pieces)
    bit = grp_size // 2
    while bit > 1:
        held = jnp.concatenate([held, swap(held, bit, 0)])
        bit //= 2
    return held, swap(held, 1, 0)


def unspread(keep, send):
    grp_size = lax.axis_size("grp")
    per = grp_size // 2
    got = swap(send, 1, 0)
    bit = grp_size // 2
    while bit > 1:
        n = keep.shape[0] // 2
        got_next = swap(half(f32(keep[n:]) + f32(got[n:])), bit, 0)
        keep = half(f32(keep[:n]) + f32(got[:n]))
        got = got_next
        bit //= 2
    size = keep.shape[0] // grp_size
    pieces = []
    for k in range(grp_size):
        rows = slice(k * size, (k + 1) * size)
        back = [(b, a) for a, b in plane_pairs(k)]
        pieces.append(lax.ppermute(half(f32(keep[rows]) + f32(got[rows])), AXES, back))
    return jnp.concatenate(pieces[:per]), jnp.concatenate(pieces[per:])


def scatter_sum(keep, send, bits):
    got = swap(send, 0, 1 << bits[0])
    for bit in bits[1:]:
        n = keep.shape[0] // 2
        got_next = swap(half(f32(keep[n:]) + f32(got[n:])), 0, 1 << bit)
        keep = half(f32(keep[:n]) + f32(got[:n]))
        got = got_next
    return f32(keep) + f32(got)


def gather(own, bits):
    held = own
    for bit in bits[:-1]:
        held = jnp.concatenate([held, swap(held, 0, 1 << bit)])
    return held, swap(held, 0, 1 << bits[-1])


def block_order(bits):
    order = [0]
    for bit in reversed(bits):
        order = order + [j ^ (1 << bit) for j in order]
    return order


def masked_dot(lhs_of, w_ref, count, turned):
    dims = (((1,), (1 if turned else 0,)), ((), ()))
    total = None
    for e in range(count):
        part = lax.dot_general(lhs_of(e), w_ref[e], dims, preferred_element_type=jnp.float32)
        total = part if total is None else total + part
    return total


def first_body(geo, turned, ids, where_ref, held_ref, got_ref, *refs):
    grp_size, ep_size, tok, stored, count, order = geo
    id_ref = refs[0] if not ids else None
    w_ref, keep_ref, send_ref, rows_ref = refs[-4:]
    per = grp_size // 2
    sub = tok // per
    bits = grp_size.bit_length() - 1
    shift = where_ref[0] ^ (where_ref[1] // 2)
    for place, j in enumerate(order):
        for s in range(per):
            k = (j & 1) * per + s
            m = shift ^ ((j >> 1) ^ k)
            at = 0
            for b in range(bits - 1):
                at = at + (((m >> (bits - 1 - b)) & 1) << b)
            src = pl.ds(pl.multiple_of((at * grp_size + k) * sub, sub), sub)
            rows = jnp.where((m & 1) == 0, held_ref[src, :], got_ref[src, :])
            rows_ref[j * tok + s * sub : j * tok + (s + 1) * sub, :] = rows
    n = len(order) // 2
    for place, j in enumerate(order):
        out_ref = keep_ref if place < n else send_ref
        at = (place % n) * tok
        rows = rows_ref[j * tok : (j + 1) * tok, :]
        if ids:
            expert = rows[:, stored : stored + 1]
        else:
            expert = id_ref[j * tok : (j + 1) * tok, :][:, stored % 128 : stored % 128 + 1]
        rows = rows[:, :stored]
        total = masked_dot(
            lambda e: jnp.where(expert == e, rows, jnp.zeros((), BF16)), w_ref, count, turned
        )
        out_ref[at : at + tok, :] = half(total)


def matmul_body(geo, turned, id_ref, rows_ref, w_ref, keep_ref, send_ref):
    tok, stored, count, order = geo
    n = len(order) // 2
    for place, j in enumerate(order):
        out_ref = keep_ref if place < n else send_ref
        at = (place % n) * tok
        rows = rows_ref[j * tok : (j + 1) * tok, :stored]
        expert = id_ref[j * tok : (j + 1) * tok, :][:, stored % 128 : stored % 128 + 1]
        total = masked_dot(
            lambda e: jnp.where(expert == e, rows, jnp.zeros((), BF16)), w_ref, count, turned
        )
        out_ref[at : at + tok, :] = half(total)


def back_body(geo, turned, where_ref, id_ref, *refs):
    grp_size, tok, stored, count, orders = geo
    keep_ref, send_ref = refs[-2:]
    per = grp_size // 2
    sub = tok // per
    shift = where_ref[0] ^ (where_ref[1] // 2)
    zero = jnp.zeros((), BF16)
    for j in range(len(orders[0])):
        expert = id_ref[j * tok : (j + 1) * tok, :][:, stored % 128 : stored % 128 + 1]
        total = None
        for i, order in enumerate(orders):
            held_ref, got_ref, w_ref = refs[3 * i : 3 * i + 3]
            n = len(order) // 2
            place = order.index(j)
            src = held_ref if place < n else got_ref
            rows = src[(place % n) * tok : (place % n + 1) * tok, :]
            part = masked_dot(
                lambda e: jnp.where(expert == e, rows, zero), w_ref, count, turned
            )
            total = part if total is None else total + part
        total = half(total)
        for s in range(per):
            k = (j & 1) * per + s
            m = shift ^ ((j >> 1) ^ k)
            dst = pl.ds(pl.multiple_of(((m >> 1) * grp_size + k) * sub, sub), sub)

            @pl.when((m & 1) == 0)
            def _():
                keep_ref[dst, :] = total[s * sub : (s + 1) * sub]

            @pl.when((m & 1) == 1)
            def _():
                send_ref[dst, :] = total[s * sub : (s + 1) * sub]


def grad_body(geo, swapped, id_ref, rows_ref, held_ref, got_ref, out_ref):
    tok, stored, order = geo
    expert = half(pl.program_id(0).astype(jnp.float32))
    n = len(order) // 2
    total = None
    for part, src in enumerate((held_ref, got_ref)):
        seq = order[part * n : (part + 1) * n]
        rows = jnp.concatenate([rows_ref[j * tok : (j + 1) * tok, :stored] for j in seq])
        ident = jnp.concatenate(
            [id_ref[j * tok : (j + 1) * tok, :][:, stored % 128 : stored % 128 + 1] for j in seq]
        )
        rows = jnp.where(ident == expert, rows, jnp.zeros((), BF16))
        pair = (src[...], rows) if swapped else (rows, src[...])
        now = lax.dot_general(*pair, (((0,), (0,)), ((), ())), preferred_element_type=jnp.float32)
        total = now if total is None else total + now
    out_ref[0] = half(total)


def cost(flops, nbytes):
    return pl.CostEstimate(flops=flops, bytes_accessed=nbytes, transcendentals=0)


def shards(tokens, routes, route_weights, hot_experts, w_gate, w_up, w_down, cotangent):
    grp_size, ep_size = lax.axis_size("grp"), lax.axis_size("ep")
    g, p = lax.axis_index("grp"), lax.axis_index("ep")
    y = p % 2
    tok = tokens.shape[0]
    count, stored, hidden = w_gate.shape
    total = tok * ep_size
    width = (stored // 128 + 1) * 128
    bits = list(range(ep_size.bit_length() - 1))
    y_first, y_last = bits, bits[1:] + bits[:1]
    where = jnp.stack([g, p]).astype(jnp.int32)
    slot_host = jnp.concatenate([jnp.arange(count, dtype=jnp.int32), hot_experts])
    slots = jnp.arange(slot_host.shape[0], dtype=jnp.int32)
    expert = jnp.sum(jnp.where(routes == slots[None, :], slot_host[None, :], 0), axis=1)
    flops = 2 * total * count * stored * hidden
    one_cost = cost(flops, 2 * (total * (stored + hidden) + count * stored * hidden))

    def halves(rows):
        first, second = rows[:, :stored], rows[:, stored:]
        return jnp.where(y == 0, first, second), jnp.where(y == 0, second, first)

    ident = half(f32(expert))[:, None]
    pad = jnp.zeros((tok, width - stored - 1), BF16)
    x_held, x_got = spread(*[jnp.concatenate([h, ident, pad], axis=1) for h in halves(tokens)])
    dz_held, dz_got = spread(*halves(half(f32(cotangent) * route_weights)))

    split = [jax.ShapeDtypeStruct((total // 2, hidden), BF16)] * 2
    id_spec = pl.BlockSpec((total, 128), lambda *_: (0, stored // 128))
    full = lambda shape: pl.BlockSpec(shape, lambda *_: (0,) * len(shape))
    first_order = block_order(y_first)
    gate_keep, gate_send, x_rows = pl.pallas_call(
        functools.partial(
            first_body, (grp_size, ep_size, tok, stored, count, first_order), False, True
        ),
        out_shape=split + [jax.ShapeDtypeStruct((total, width), BF16)],
        in_specs=[SMEM, VMEM, VMEM, VMEM],
        out_specs=[VMEM] * 3,
        compiler_params=PARAMS,
        cost_estimate=one_cost,
        name="gate_rows",
    )(where, x_held, x_got, w_gate)
    up_keep, up_send = pl.pallas_call(
        functools.partial(matmul_body, (tok, stored, count, first_order), False),
        out_shape=split,
        grid=(1,),
        in_specs=[id_spec, full((total, width)), full(w_up.shape)],
        out_specs=[full((total // 2, hidden))] * 2,
        compiler_params=PARAMS,
        cost_estimate=one_cost,
        name="up_rows",
    )(x_rows, x_rows, w_up)
    ag_keep, ag_send, dz_rows = pl.pallas_call(
        functools.partial(
            first_body, (grp_size, ep_size, tok, stored, count, block_order(y_last)), True, False
        ),
        out_shape=split + [jax.ShapeDtypeStruct((total, stored), BF16)],
        grid=(1,),
        in_specs=[SMEM, full(dz_held.shape), full(dz_got.shape), id_spec, full(w_down.shape)],
        out_specs=[full((total // 2, hidden))] * 2 + [full((total, stored))],
        compiler_params=PARAMS,
        cost_estimate=one_cost,
        name="act_grad_rows",
    )(where, dz_held, dz_got, x_rows, w_down)

    gate_pre = scatter_sum(gate_keep, gate_send, y_first)
    up_pre = scatter_sum(up_keep, up_send, y_first)
    act_grad = scatter_sum(ag_keep, ag_send, y_last)
    sg = jax.nn.sigmoid(gate_pre)
    act = half(gate_pre * sg * up_pre)
    gate_grad = half(act_grad * up_pre * sg * (1.0 + gate_pre * (1.0 - sg)))
    up_grad = half(act_grad * gate_pre * sg)

    late, early = y_first[::-1], y_last[::-1]
    late_order, early_order = block_order(y_first), block_order(y_last)
    act_held, act_got = gather(act, late)
    gg_held, gg_got = gather(gate_grad, late)
    ug_held, ug_got = gather(up_grad, early)

    back_shape = [jax.ShapeDtypeStruct((total // 2, stored), BF16)] * 2
    half_spec = full((total // 2, hidden))

    def back(orders, turned, name, *args):
        return pl.pallas_call(
            functools.partial(back_body, (grp_size, tok, stored, count, orders), turned),
            out_shape=back_shape,
            grid=(1,),
            in_specs=[SMEM, id_spec]
            + [spec for i in range(len(orders)) for spec in (half_spec, half_spec, full(args[3 * i + 2].shape))],
            out_specs=[full((total // 2, stored))] * 2,
            compiler_params=PARAMS,
            cost_estimate=cost(flops * len(orders), one_cost.bytes_accessed * len(orders)),
            name=name,
        )(where, x_rows, *args)

    def grad(rows, held, got, order, swapped, name):
        shape = (hidden, stored) if swapped else (stored, hidden)
        return pl.pallas_call(
            functools.partial(grad_body, (tok, stored, order), swapped),
            out_shape=jax.ShapeDtypeStruct((count,) + shape, BF16),
            grid=(count,),
            in_specs=[id_spec, full(rows.shape), half_spec, half_spec],
            out_specs=pl.BlockSpec((1,) + shape, lambda e: (e, 0, 0)),
            compiler_params=PARAMS,
            cost_estimate=one_cost,
            name=name,
        )(x_rows, rows, held, got)

    out_keep, out_send = back([late_order], False, "out_rows", act_held, act_got, w_down)
    mine, other = unspread(out_keep, out_send)

    def joined(mine, other):
        return jnp.concatenate(
            [jnp.where(y == 0, mine, other), jnp.where(y == 0, other, mine)], axis=1
        )

    layer_output = half(f32(joined(mine, other)) * route_weights)
    tok_keep, tok_send = back(
        [late_order, early_order], True, "token_rows", gg_held, gg_got, w_gate, ug_held, ug_got, w_up
    )
    grad_tokens = joined(*unspread(tok_keep, tok_send))
    grad_down = grad(dz_rows, act_held, act_got, late_order, True, "grad_down")
    grad_gate = grad(x_rows, gg_held, gg_got, late_order, False, "grad_gate")
    grad_up = grad(x_rows, ug_held, ug_got, early_order, False, "grad_up")
    return (layer_output, grad_tokens, grad_gate, grad_up, grad_down)


def solution(mesh):
    placed = (
        P("ep", "grp"),
        P("ep", None),
        P("ep", None),
        P(),
        P(None, "ep", "grp"),
        P(None, "ep", "grp"),
        P(None, "grp", "ep"),
        P("ep", "grp"),
    )
    return jax.shard_map(
        shards,
        mesh=mesh,
        in_specs=placed,
        out_specs=(
            P("ep", "grp"),
            P("ep", "grp"),
            P(None, "ep", "grp"),
            P(None, "ep", "grp"),
            P(None, "grp", "ep"),
        ),
        check_vma=False,
    )
```

```python
import functools

import jax
import jax.numpy as jnp
from jax import lax
from jax.experimental import pallas as pl
from jax.experimental.pallas import tpu as pltpu
from jax.sharding import PartitionSpec as P

AXES = ("grp", "ep")
BF16 = jnp.bfloat16
VMEM = pl.BlockSpec(memory_space=pltpu.VMEM)
SMEM = pl.BlockSpec(memory_space=pltpu.SMEM)
PARAMS = pltpu.CompilerParams(vmem_limit_bytes=50 * 1024 * 1024)
PARTS = 2


def f32(a):
    return a.astype(jnp.float32)


def half(a):
    return a.astype(BF16)


def after(value, *others):
    return lax.optimization_barrier((value,) + others)[0]


def swap(block, grp_bits, ep_bits):
    grp_size, ep_size = lax.axis_size("grp"), lax.axis_size("ep")
    pairs = [
        (g * ep_size + p, (g ^ grp_bits) * ep_size + (p ^ ep_bits))
        for g in range(grp_size)
        for p in range(ep_size)
    ]
    return lax.ppermute(block, AXES, pairs)


def plane_pairs(k):
    grp_size, ep_size = lax.axis_size("grp"), lax.axis_size("ep")
    flip = k * (grp_size // 2)
    return [
        (g * ep_size + p, ((p // 2) ^ flip) * ep_size + 2 * g + ((p % 2) ^ k))
        for g in range(grp_size)
        for p in range(ep_size)
    ]


def spread(pieces):
    grp_size = lax.axis_size("grp")
    landed = [lax.ppermute(pieces[k], AXES, plane_pairs(k)) for k in range(2)]
    held = jnp.concatenate(landed)
    bit = grp_size // 2
    while bit > 1:
        held = jnp.concatenate([held, swap(held, bit, 0)])
        bit //= 2
    return held, swap(held, 1, 0), landed[0]


def unspread(keep, send):
    grp_size = lax.axis_size("grp")
    got = swap(send, 1, 0)
    marks = []
    bit = grp_size // 2
    while bit > 1:
        n = keep.shape[0] // 2
        out = half(f32(keep[n:]) + f32(got[n:]))
        marks.append(out)
        got_next = swap(out, bit, 0)
        keep = half(f32(keep[:n]) + f32(got[:n]))
        got = got_next
        bit //= 2
    size = keep.shape[0] // 2
    pieces = []
    for k in range(2):
        rows = slice(k * size, (k + 1) * size)
        back = [(b, a) for a, b in plane_pairs(k)]
        out = half(f32(keep[rows]) + f32(got[rows]))
        marks.append(out)
        pieces.append(lax.ppermute(out, AXES, back))
    return pieces, marks


def scatter_sum(keep, send, bits):
    got = swap(send, 0, 1 << bits[0])
    for bit in bits[1:]:
        n = keep.shape[0] // 2
        got_next = swap(half(f32(keep[n:]) + f32(got[n:])), 0, 1 << bit)
        keep = half(f32(keep[:n]) + f32(got[:n]))
        got = got_next
    return f32(keep) + f32(got)


def gather(own, bits):
    held = own
    for bit in bits[:-1]:
        held = jnp.concatenate([held, swap(held, 0, 1 << bit)])
    return held, swap(held, 0, 1 << bits[-1])


def block_order(bits):
    order = [0]
    for bit in reversed(bits):
        order = order + [j ^ (1 << bit) for j in order]
    return order


def upright(row):
    n = row.shape[1]
    at = lax.broadcasted_iota(jnp.int32, (n, n), 0) == lax.broadcasted_iota(jnp.int32, (n, n), 1)
    return jnp.sum(jnp.where(at, row, jnp.zeros((), row.dtype)), axis=1, keepdims=True)


def cut_body(stored, count, hot_ref, routes_ref, tokens_ref, own_ref, other_ref):
    y = lax.axis_index("ep") % 2
    slot = upright(routes_ref[...])
    expert = slot
    for r in range(hot_ref.shape[0]):
        expert = jnp.where(slot == count + r, hot_ref[r], expert)
    lane = lax.broadcasted_iota(jnp.int32, (slot.shape[0], own_ref.shape[1] - stored), 1)
    tail = half(jnp.where(lane == 0, f32(expert), 0.0))
    rows = tokens_ref[...]
    first, second = rows[:, :stored], rows[:, stored:]
    own_ref[:, :stored] = jnp.where(y == 0, first, second)
    own_ref[:, stored:] = tail
    other_ref[:, :stored] = jnp.where(y == 0, second, first)
    other_ref[:, stored:] = tail


def weigh_body(stored, weights_ref, rows_ref, own_ref, other_ref):
    y = lax.axis_index("ep") % 2
    rows = half(f32(rows_ref[...]) * upright(weights_ref[...]))
    tail = jnp.zeros((rows.shape[0], own_ref.shape[1] - stored), BF16)
    first, second = rows[:, :stored], rows[:, stored:]
    own_ref[:, :stored] = jnp.where(y == 0, first, second)
    own_ref[:, stored:] = tail
    other_ref[:, :stored] = jnp.where(y == 0, second, first)
    other_ref[:, stored:] = tail


def order_rows(geo, held_ref, got_ref, rows_ref):
    grp_size, tok, order = geo
    sub = tok // PARTS
    bits = grp_size.bit_length() - 1
    shift = lax.axis_index("grp") ^ (lax.axis_index("ep") // 2)
    for place, j in enumerate(order):
        k = j & 1
        m = shift ^ ((j >> 1) ^ (k * (grp_size // 2)))
        at = 0
        for b in range(bits - 1):
            at = at + (((m >> (bits - 1 - b)) & 1) << b)
        src = pl.ds(pl.multiple_of((at * 2 + k) * tok, tok), tok)
        rows = jnp.where((m & 1) == 0, held_ref[src, :], got_ref[src, :])
        for part in range(PARTS):
            to = (part * len(order) + place) * sub
            rows_ref[to : to + sub, :] = rows[part * sub : (part + 1) * sub]


def expert_dot(rows, expert, w_ref, count, turned):
    dims = (((1,), (1 if turned else 0,)), ((), ()))
    total = None
    for e in range(count):
        own = jnp.where(expert == e, rows, jnp.zeros((), BF16))
        part = lax.dot_general(own, w_ref[e], dims, preferred_element_type=jnp.float32)
        total = part if total is None else total + part
    return total


def id_of(id_ref, stored, rows):
    return id_ref[rows, :][:, stored % 128 : stored % 128 + 1]


def first_body(geo, stored, count, n_w, own_ids, held_ref, got_ref, *refs):
    rows_ref = refs[-1]
    order_rows(geo, held_ref, got_ref, rows_ref)
    n = rows_ref.shape[0] // PARTS
    rows = rows_ref[:n, :]
    if own_ids:
        expert = rows[:, stored : stored + 1]
        refs = refs[:-1]
    else:
        expert = id_of(refs[0], stored, slice(0, n))
        refs = refs[1:-1]
    products(rows[:, :stored], expert, count, n_w, refs)


def products(rows, expert, count, n_w, refs):
    keep_ref, send_ref = refs[-2:]
    n = rows.shape[0] // 2
    hidden = keep_ref.shape[1] // n_w
    for i in range(n_w):
        result = half(expert_dot(rows, expert, refs[i], count, False))
        cols = slice(i * hidden, (i + 1) * hidden)
        keep_ref[:, cols] = result[:n]
        send_ref[:, cols] = result[n:]


def later_body(stored, count, n_w, id_ref, rows_ref, *refs):
    expert = id_of(id_ref, stored, slice(None))
    products(rows_ref[:, :stored], expert, count, n_w, refs)


def back_body(geo, stored, count, n_w, id_ref, *refs):
    grp_size, tok, order = geo
    keep_ref, send_ref = refs[-2:]
    sub = tok // PARTS
    shift = lax.axis_index("grp") ^ (lax.axis_index("ep") // 2)
    n = len(order) // 2
    for part in range(PARTS):
        for side in range(2):
            src = refs[n_w + 2 * part + side]
            hidden = src.shape[1] // n_w
            at = (part * 2 + side) * n * sub
            expert = id_of(id_ref, stored, slice(at, at + n * sub))
            total = None
            for i in range(n_w):
                rows = src[:, i * hidden : (i + 1) * hidden]
                now = expert_dot(rows, expert, refs[i], count, True)
                total = now if total is None else total + now
            total = half(total)
            for place in range(n):
                j = order[side * n + place]
                k = j & 1
                m = shift ^ ((j >> 1) ^ (k * (grp_size // 2)))
                to = ((m >> 1) * 2 + k) * tok + part * sub
                to = pl.ds(pl.multiple_of(to, sub), sub)
                block = total[place * sub : (place + 1) * sub]

                @pl.when((m & 1) == 0)
                def _():
                    keep_ref[to, :] = block

                @pl.when((m & 1) == 1)
                def _():
                    send_ref[to, :] = block


def grad_body(stored, cols, id_ref, rows_ref, *refs):
    out_ref = refs[-1]
    expert = half(pl.program_id(0).astype(jnp.float32))
    right = jnp.concatenate([ref[:, cols] for ref in refs[:-1]])
    right = jnp.where(id_of(id_ref, stored, slice(None)) == expert, right, jnp.zeros((), BF16))
    out_ref[0] = half(
        lax.dot_general(
            rows_ref[:, :stored],
            right,
            (((0,), (0,)), ((), ())),
            preferred_element_type=jnp.float32,
        )
    )


def cost(flops, nbytes):
    return pl.CostEstimate(flops=flops, bytes_accessed=nbytes, transcendentals=0)


def full(shape):
    return pl.BlockSpec(shape, lambda *_: (0,) * len(shape))


def shards(tokens, routes, route_weights, hot_experts, w_gate, w_up, w_down, cotangent):
    grp_size, ep_size = lax.axis_size("grp"), lax.axis_size("ep")
    y = lax.axis_index("ep") % 2
    tok = tokens.shape[0]
    w_down = jnp.swapaxes(w_down, 1, 2)
    count, stored, hidden = w_gate.shape
    total = tok * ep_size
    n = total // PARTS
    width = (stored // 128 + 1) * 128
    bits = list(range(ep_size.bit_length() - 1))
    order = block_order(bits)
    geo = (grp_size, tok, order)
    flops = 2 * total * count * stored * hidden
    nbytes = 2 * (total * (stored + hidden) + count * stored * hidden)
    piece = [jax.ShapeDtypeStruct((tok, width), BF16)] * 2

    def call(body, out_shape, args, in_specs=None, part=1.0, name=None, **kw):
        return pl.pallas_call(
            body,
            out_shape=out_shape,
            grid=kw.get("grid", (1,)),
            in_specs=in_specs or [full(a.shape) for a in args],
            out_specs=kw.get("out_specs") or [full(o.shape) for o in out_shape],
            compiler_params=PARAMS,
            cost_estimate=cost(int(flops * part), int(nbytes * part)),
            name=name,
        )(*args)

    x_pieces = call(
        functools.partial(cut_body, stored, count),
        piece,
        (hot_experts, routes.reshape(1, tok), tokens),
        in_specs=[SMEM, full((1, tok)), full(tokens.shape)],
        part=0.01,
        name="token_pieces",
    )
    x_held, x_got, landed = spread(x_pieces)
    cot, _ = lax.optimization_barrier((cotangent, landed))
    dz_pieces = call(
        functools.partial(weigh_body, stored),
        piece,
        (route_weights.reshape(1, tok), cot),
        part=0.01,
        name="cotangent_pieces",
    )
    dz_held, dz_got, _ = spread(dz_pieces)

    rows_shape = jax.ShapeDtypeStruct((total, width), BF16)

    def id_spec(rows, at):
        return pl.BlockSpec((rows, 128), lambda *_: (at, stored // 128))

    def split(n_w):
        return [jax.ShapeDtypeStruct((n // 2, n_w * hidden), BF16)] * 2

    def later(part, rows, weights, name):
        return call(
            functools.partial(later_body, stored, count, len(weights)),
            split(len(weights)),
            (x_rows, rows) + weights,
            in_specs=[
                id_spec(n, part),
                pl.BlockSpec((n, width), lambda *_: (part, 0)),
            ]
            + [full(w.shape) for w in weights],
            part=len(weights) / PARTS,
            name=name,
        )

    gu_keep, gu_send, x_rows = call(
        functools.partial(first_body, geo, stored, count, 2, True),
        split(2) + [rows_shape],
        (x_held, x_got, w_gate, w_up),
        part=2 / PARTS,
        name="gate_up_first",
    )
    ag_keep, ag_send, dz_rows = call(
        functools.partial(first_body, geo, stored, count, 1, False),
        split(1) + [rows_shape],
        (dz_held, dz_got, x_rows, w_down),
        in_specs=[full(dz_held.shape), full(dz_got.shape), id_spec(total, 0), full(w_down.shape)],
        part=1 / PARTS,
        name="act_grad_first",
    )
    gate_up = [(gu_keep, gu_send)]
    act_grad = [(ag_keep, ag_send)]
    mark = ag_send
    for part in range(1, PARTS):
        gate_up.append(later(part, after(x_rows, mark), (w_gate, w_up), "gate_up_later"))
        act_grad.append(later(part, after(dz_rows, gate_up[-1][1]), (w_down,), "act_grad_later"))
        mark = act_grad[-1][1]

    acts, grads = [], []
    for part in range(PARTS):
        gu = scatter_sum(*gate_up[part], bits)
        ag = scatter_sum(*act_grad[part], bits)
        gate_pre, up_pre = gu[:, :hidden], gu[:, hidden:]
        sg = jax.nn.sigmoid(gate_pre)
        act = half(gate_pre * sg * up_pre)
        gate_grad = ag * up_pre * sg * (1.0 + gate_pre * (1.0 - sg))
        up_grad = ag * gate_pre * sg
        both = half(jnp.concatenate([gate_grad, up_grad], axis=1))
        acts.extend(gather(act, bits[::-1]))
        grads.extend(gather(both, bits[::-1]))

    def back(n_w, weights, gathered, name):
        return call(
            functools.partial(back_body, geo, stored, count, n_w),
            [jax.ShapeDtypeStruct((total // 2, stored), BF16)] * 2,
            (x_rows,) + weights + tuple(gathered),
            in_specs=[id_spec(total, 0)] + [full(a.shape) for a in weights + tuple(gathered)],
            part=n_w,
            name=name,
        )

    def grad(rows, gathered, at, name):
        return call(
            functools.partial(grad_body, stored, slice(at * hidden, (at + 1) * hidden)),
            jax.ShapeDtypeStruct((count, stored, hidden), BF16),
            (x_rows, rows) + tuple(gathered),
            in_specs=[id_spec(total, 0)] + [full(a.shape) for a in (rows,) + tuple(gathered)],
            grid=(count,),
            out_specs=pl.BlockSpec((1, stored, hidden), lambda e: (e, 0, 0)),
            name=name,
        )

    def joined(mine, other):
        return jnp.concatenate(
            [jnp.where(y == 0, mine, other), jnp.where(y == 0, other, mine)], axis=1
        )

    pieces, _ = unspread(*back(1, (w_down,), acts, "out_rows"))
    layer_output = half(f32(joined(*pieces)) * route_weights)
    tok_keep, tok_send = back(2, (w_gate, w_up), grads, "token_rows")
    pieces, marks = unspread(tok_keep, tok_send)
    grad_tokens = joined(*pieces)
    grad_down = grad(after(dz_rows, tok_send), acts, 0, "grad_down")
    grad_gate = grad(after(x_rows, marks[0]), grads, 0, "grad_gate")
    grad_up = grad(after(x_rows, *marks), grads, 1, "grad_up")
    return (layer_output, grad_tokens, grad_gate, grad_up, jnp.swapaxes(grad_down, 1, 2))


def solution(mesh):
    placed = (
        P("ep", "grp"),
        P("ep", None),
        P("ep", None),
        P(),
        P(None, "ep", "grp"),
        P(None, "ep", "grp"),
        P(None, "grp", "ep"),
        P("ep", "grp"),
    )
    return jax.shard_map(
        shards,
        mesh=mesh,
        in_specs=placed,
        out_specs=(
            P("ep", "grp"),
            P("ep", "grp"),
            P(None, "ep", "grp"),
            P(None, "ep", "grp"),
            P(None, "grp", "ep"),
        ),
        check_vma=False,
    )
```

```python
import functools

import jax
import jax.numpy as jnp
from jax import lax
from jax.experimental import pallas as pl
from jax.experimental.pallas import tpu as pltpu
from jax.sharding import PartitionSpec as P

AXES = ("grp", "ep")
BF16 = jnp.bfloat16
VMEM = pl.BlockSpec(memory_space=pltpu.VMEM)
SMEM = pl.BlockSpec(memory_space=pltpu.SMEM)
PARAMS = pltpu.CompilerParams(vmem_limit_bytes=50 * 1024 * 1024)
PARTS = 2


def f32(a):
    return a.astype(jnp.float32)


def half(a):
    return a.astype(BF16)


def after(value, *others):
    return lax.optimization_barrier((value,) + others)[0]


def swap(block, grp_bits, ep_bits):
    grp_size, ep_size = lax.axis_size("grp"), lax.axis_size("ep")
    pairs = [
        (g * ep_size + p, (g ^ grp_bits) * ep_size + (p ^ ep_bits))
        for g in range(grp_size)
        for p in range(ep_size)
    ]
    return lax.ppermute(block, AXES, pairs)


def plane_pairs(k):
    grp_size, ep_size = lax.axis_size("grp"), lax.axis_size("ep")
    flip = k * (grp_size // 2)
    return [
        (g * ep_size + p, ((p // 2) ^ flip) * ep_size + 2 * g + ((p % 2) ^ k))
        for g in range(grp_size)
        for p in range(ep_size)
    ]


def column_pairs(across):
    grp_size, ep_size = lax.axis_size("grp"), lax.axis_size("ep")
    top = grp_size // 2
    pairs = []
    for g in range(grp_size):
        for p in range(ep_size):
            z = p // 2
            k = 1 if (g ^ z) & top else 0
            source = g ^ (top if k ^ across else 0)
            target = z ^ (k * top)
            pairs.append((g * ep_size + p, target * ep_size + 2 * source + ((p % 2) ^ k)))
    return pairs


def crossing():
    top = lax.axis_size("grp") // 2
    apart = (lax.axis_index("grp") ^ (lax.axis_index("ep") // 2)) & top
    return (apart != 0).astype(jnp.int32)


class Line:
    def __init__(self):
        self.last = None

    def begin(self, *values):
        if self.last is None:
            return values
        return lax.optimization_barrier(values + (self.last,))[:-1]

    def end(self, value):
        self.last = value
        return value


def summed(terms, rows):
    return functools.reduce(lambda a, b: a + b, [f32(term[rows]) for term in terms])


class Sum:
    def __init__(self, line, keep, send, swaps):
        self.line, self.swaps = line, list(swaps)
        self.terms = [keep]
        self.got = self.swaps.pop(0)(send)

    def fold(self):
        n = self.got.shape[0] // 2
        self.terms[0], self.got = self.line.begin(self.terms[0], self.got)
        terms = self.terms + [self.got]
        send = self.line.end(half(summed(terms, slice(n, None))))
        self.terms = [term[:n] for term in terms]
        self.got = self.swaps.pop(0)(send)

    def finish(self):
        self.terms[0], self.got = self.line.begin(self.terms[0], self.got)
        self.total = self.line.end(summed(self.terms + [self.got], slice(None)))


class Gather:
    def __init__(self, line, own, swaps):
        self.line, self.swaps = line, list(swaps)
        self.held = own
        self.got = self.swaps.pop(0)(own)

    def grow(self):
        held, got = self.line.begin(self.held, self.got)
        self.held = self.line.end(jnp.concatenate([held, got]))
        self.got = self.swaps.pop(0)(self.held)

    def result(self):
        return [self.held, self.got]


class Return:
    def __init__(self, line, keep, send):
        bits = lax.axis_size("grp").bit_length() - 1
        swaps = [functools.partial(swap, grp_bits=1, ep_bits=0)]
        for bit in range(bits - 1, 0, -1):
            swaps.append(functools.partial(swap, grp_bits=1 << bit, ep_bits=0))
        self.rounds = bits - 1
        self.line = line
        self.sum = Sum(line, keep, send, swaps)

    def fold(self):
        self.sum.fold()

    def leave(self):
        total = self.sum
        total.terms[0], total.got = self.line.begin(total.terms[0], total.got)
        n = total.got.shape[0] // 2
        self.pieces = []
        for k in range(2):
            back = [(b, a) for a, b in plane_pairs(k)]
            piece = half(summed(total.terms + [total.got], slice(k * n, (k + 1) * n)))
            self.line.end(piece)
            self.pieces.append(lax.ppermute(piece, AXES, back))


def block_order(bits):
    order = [0]
    for bit in reversed(bits):
        order = order + [j ^ (1 << bit) for j in order]
    return order


def upright(row):
    n = row.shape[1]
    at = lax.broadcasted_iota(jnp.int32, (n, n), 0) == lax.broadcasted_iota(jnp.int32, (n, n), 1)
    return jnp.sum(jnp.where(at, row, jnp.zeros((), row.dtype)), axis=1, keepdims=True)


def cut_body(stored, count, hot_ref, routes_ref, tokens_ref, own_ref, other_ref):
    y = (lax.axis_index("ep") % 2) ^ crossing()
    slot = upright(routes_ref[...])
    expert = slot
    for r in range(hot_ref.shape[0]):
        expert = jnp.where(slot == count + r, hot_ref[r], expert)
    lane = lax.broadcasted_iota(jnp.int32, (slot.shape[0], own_ref.shape[1] - stored), 1)
    tail = half(jnp.where(lane == 0, f32(expert), 0.0))
    rows = tokens_ref[...]
    first, second = rows[:, :stored], rows[:, stored:]
    own_ref[:, :stored] = jnp.where(y == 0, first, second)
    own_ref[:, stored:] = tail
    other_ref[:, :stored] = jnp.where(y == 0, second, first)
    other_ref[:, stored:] = tail


def weigh_body(stored, weights_ref, rows_ref, own_ref, other_ref):
    y = (lax.axis_index("ep") % 2) ^ crossing()
    rows = half(f32(rows_ref[...]) * upright(weights_ref[...]))
    tail = jnp.zeros((rows.shape[0], own_ref.shape[1] - stored), BF16)
    first, second = rows[:, :stored], rows[:, stored:]
    own_ref[:, :stored] = jnp.where(y == 0, first, second)
    own_ref[:, stored:] = tail
    other_ref[:, :stored] = jnp.where(y == 0, second, first)
    other_ref[:, stored:] = tail


def order_rows(geo, held_ref, got_ref, rows_ref):
    grp_size, tok, order = geo
    sub = tok // PARTS
    bits = grp_size.bit_length() - 1
    shift = lax.axis_index("grp") ^ (lax.axis_index("ep") // 2)
    for place, j in enumerate(order):
        k = j & 1
        m = shift ^ ((j >> 1) ^ (k * (grp_size // 2)))
        at = 0
        for b in range(bits - 1):
            at = at + (((m >> (bits - 1 - b)) & 1) << b)
        landed = 1 if (j >> 1) & (grp_size // 2) else 0
        src = pl.ds(pl.multiple_of((at * 2 + landed) * tok, tok), tok)
        rows = jnp.where((m & 1) == 0, held_ref[src, :], got_ref[src, :])
        for part in range(PARTS):
            to = (part * len(order) + place) * sub
            rows_ref[to : to + sub, :] = rows[part * sub : (part + 1) * sub]


def expert_dot(rows, expert, w_ref, count, turned):
    zero = jnp.zeros((), BF16)
    own = jnp.concatenate([jnp.where(expert == e, rows, zero) for e in range(count)], axis=1)
    if turned:
        weights = jnp.concatenate([w_ref[e] for e in range(count)], axis=1)
    else:
        weights = w_ref[...].reshape(own.shape[1], w_ref.shape[2])
    dims = (((1,), (1 if turned else 0,)), ((), ()))
    return lax.dot_general(own, weights, dims, preferred_element_type=jnp.float32)


def id_of(id_ref, stored, rows):
    return id_ref[rows, :][:, stored % 128 : stored % 128 + 1]


def first_body(geo, stored, count, n_w, own_ids, held_ref, got_ref, *refs):
    rows_ref = refs[-1]
    order_rows(geo, held_ref, got_ref, rows_ref)
    n = rows_ref.shape[0] // PARTS
    rows = rows_ref[:n, :]
    if own_ids:
        expert = rows[:, stored : stored + 1]
        refs = refs[:-1]
    else:
        expert = id_of(refs[0], stored, slice(0, n))
        refs = refs[1:-1]
    products(rows[:, :stored], expert, count, n_w, refs)


def products(rows, expert, count, n_w, refs, places=None):
    keep_ref, send_ref = refs[-2:]
    n = rows.shape[0] // 2
    hidden = keep_ref.shape[1] // n_w
    places = places or (0, 1)
    size = rows.shape[0] // len(places)
    for i in range(n_w):
        result = half(expert_dot(rows, expert, refs[i], count, False))
        cols = slice(i * hidden, (i + 1) * hidden)
        for block, place in enumerate(places):
            out_ref, at = (keep_ref, place * size) if place * size < n else (send_ref, place * size - n)
            out_ref[at : at + size, cols] = result[block * size : (block + 1) * size]


def later_body(stored, count, n_w, places, id_ref, rows_ref, *refs):
    expert = id_of(id_ref, stored, slice(None))
    products(rows_ref[:, :stored], expert, count, n_w, refs, places)


def in_order(held, got, source, order):
    n = len(source) // 2
    sub = held.shape[0] // n
    if source == order:
        return [held, got]
    blocks = []
    for j in order:
        place = source.index(j)
        half_of = held if place < n else got
        blocks.append(half_of[(place % n) * sub : (place % n + 1) * sub])
    return [jnp.concatenate(blocks[:n]), jnp.concatenate(blocks[n:])]


def back_body(geo, stored, count, jobs, id_ref, *refs):
    grp_size, tok, order = geo
    keep_ref, send_ref = refs[-2:]
    sub = tok // PARTS
    shift = lax.axis_index("grp") ^ (lax.axis_index("ep") // 2)
    n = len(order) // 2
    for number, (part, terms) in enumerate(jobs):
        for side in range(2):
            at = (part * 2 + side) * n * sub
            expert = id_of(id_ref, stored, slice(at, at + n * sub))
            total = None
            for weight, pair, col, source in terms:
                hidden = refs[weight].shape[2]
                cols = slice(col * hidden, (col + 1) * hidden)
                rows = in_order(refs[pair][:, cols], refs[pair + 1][:, cols], source, order)[side]
                now = expert_dot(rows, expert, refs[weight], count, True)
                total = now if total is None else total + now
            total = half(total)
            for place in range(n):
                j = order[side * n + place]
                k = j & 1
                m = shift ^ ((j >> 1) ^ (k * (grp_size // 2)))
                to = (((m >> 1) * 2 + k) * len(jobs) + number) * sub
                to = pl.ds(pl.multiple_of(to, sub), sub)
                block = total[place * sub : (place + 1) * sub]

                @pl.when((m & 1) == 0)
                def _():
                    keep_ref[to, :] = block

                @pl.when((m & 1) == 1)
                def _():
                    send_ref[to, :] = block


def grad_body(stored, cols, sources, order, id_ref, rows_ref, *refs):
    out_ref = refs[-1]
    expert = half(pl.program_id(0).astype(jnp.float32))
    right = []
    for part, source in enumerate(sources):
        right += in_order(refs[2 * part][:, cols], refs[2 * part + 1][:, cols], source, order)
    right = jnp.concatenate(right)
    right = jnp.where(id_of(id_ref, stored, slice(None)) == expert, right, jnp.zeros((), BF16))
    out_ref[0] = half(
        lax.dot_general(
            rows_ref[:, :stored],
            right,
            (((0,), (0,)), ((), ())),
            preferred_element_type=jnp.float32,
        )
    )


def full(shape):
    return pl.BlockSpec(shape, lambda *_: (0,) * len(shape))


def shards(tokens, routes, route_weights, hot_experts, w_gate, w_up, w_down, cotangent):
    grp_size, ep_size = lax.axis_size("grp"), lax.axis_size("ep")
    y = lax.axis_index("ep") % 2
    tok = tokens.shape[0]
    w_down = jnp.swapaxes(w_down, 1, 2)
    count, stored, hidden = w_gate.shape
    total = tok * ep_size
    n = total // PARTS
    width = (stored // 128 + 1) * 128
    bits = list(range(ep_size.bit_length() - 1))
    order = block_order(bits)
    geo = (grp_size, tok, order)
    piece = [jax.ShapeDtypeStruct((tok, width), BF16)] * 2

    def call(body, out_shape, args, in_specs=None, name=None, **kw):
        return pl.pallas_call(
            body,
            out_shape=out_shape,
            grid=kw.get("grid", (1,)),
            in_specs=in_specs or [full(a.shape) for a in args],
            out_specs=kw.get("out_specs") or [full(o.shape) for o in out_shape],
            compiler_params=PARAMS,
            cost_estimate=pl.CostEstimate(flops=1, bytes_accessed=1, transcendentals=0),
            name=name,
        )(*args)

    x_pieces = call(
        functools.partial(cut_body, stored, count),
        piece,
        (hot_experts, routes.reshape(1, tok), tokens),
        in_specs=[SMEM, full((1, tok)), full(tokens.shape)],
        name="token_pieces",
    )
    line = Line()
    bit_swaps = [functools.partial(swap, grp_bits=0, ep_bits=1 << bit) for bit in bits]
    grp_bits = range(grp_size.bit_length() - 2, 0, -1)

    apart = crossing()

    def hop(pieces):
        return pieces[0], swap(pieces[1], grp_size // 2, 0)

    def land(pieces):
        stay, got = line.begin(*pieces)
        near = jnp.where(apart == 0, stay, got)
        far = line.end(jnp.where(apart == 0, got, stay))
        return [
            lax.ppermute(near, AXES, column_pairs(0)),
            lax.ppermute(far, AXES, column_pairs(1)),
        ]

    def joined_up(pieces):
        return line.end(jnp.concatenate(line.begin(*pieces)))

    dz_pieces = call(
        functools.partial(weigh_body, stored),
        piece,
        (route_weights.reshape(1, tok), cotangent),
        name="cotangent_pieces",
    )
    x_pieces, dz_pieces = hop(x_pieces), hop(dz_pieces)
    x_landed = land(x_pieces)
    dz_landed = land(dz_pieces)
    x_held, dz_held = joined_up(x_landed), None

    def widened(held):
        return [swap(held, 1 << bit, 0) for bit in grp_bits[:1]]

    def doubled(held, got):
        for i, bit in enumerate(grp_bits):
            held = joined_up((held, got[0] if i == 0 else swap(held, 1 << bit, 0)))
        return held

    x_next = widened(x_held)
    dz_held = joined_up(dz_landed)
    dz_next = widened(dz_held)
    x_held = doubled(x_held, x_next)
    x_got = swap(x_held, 1, 0)

    rows_shape = jax.ShapeDtypeStruct((total, width), BF16)

    def id_spec(rows, at):
        return pl.BlockSpec((rows, 128), lambda *_: (at, stored // 128))

    def split(n_w):
        return [jax.ShapeDtypeStruct((n // 2, n_w * hidden), BF16)] * 2

    def later(part, rows, weights, name, places=None):
        return call(
            functools.partial(later_body, stored, count, len(weights), places),
            split(len(weights)),
            (x_rows, rows) + weights,
            in_specs=[
                id_spec(n, part),
                pl.BlockSpec((n, width), lambda *_: (part, 0)),
            ]
            + [full(w.shape) for w in weights],
            name=name,
        )

    x_held, x_got = line.begin(x_held, x_got)
    gu_keep, gu_send, x_rows = call(
        functools.partial(first_body, geo, stored, count, 2, True),
        split(2) + [rows_shape],
        (x_held, x_got, w_gate, w_up),
        name="gate_up_first",
    )
    line.end(gu_send)
    gu = [Sum(line, gu_keep, gu_send, bit_swaps)]
    turned_bits = [bits[1], bits[0]] + bits[2:]
    turned_order = block_order(turned_bits)
    turned_swaps = [bit_swaps[1], bit_swaps[0]] + bit_swaps[2:]
    places = [turned_order.index(j) for j in order]
    dz_held = doubled(dz_held, dz_next)
    dz_got = swap(dz_held, 1, 0)
    (rows,) = line.begin(x_rows)
    keep, send = later(1, rows, (w_gate, w_up), "gate_up_later", places)
    line.end(send)
    gu.append(Sum(line, keep, send, turned_swaps))
    dz_held, dz_got = line.begin(dz_held, dz_got)
    ag_keep, ag_send, dz_rows = call(
        functools.partial(first_body, geo, stored, count, 1, False),
        split(1) + [rows_shape],
        (dz_held, dz_got, x_rows, w_down),
        in_specs=[full(dz_held.shape), full(dz_got.shape), id_spec(total, 0), full(w_down.shape)],
        name="act_grad_first",
    )
    line.end(ag_send)
    ag = [Sum(line, ag_keep, ag_send, bit_swaps)]
    (rows,) = line.begin(dz_rows)
    keep, send = later(1, rows, (w_down,), "act_grad_later", places)
    line.end(send)
    ag.append(Sum(line, keep, send, turned_swaps))
    acts, grads = [None] * PARTS, [None] * PARTS
    sources = [order, turned_order]
    back_swaps = [bit_swaps[::-1], turned_swaps[::-1]]

    def middle(part):
        ag[part].finish()
        gate_up, act_grad = gu[part].total, ag[part].total
        gate_pre, up_pre = gate_up[:, :hidden], gate_up[:, hidden:]
        sg = jax.nn.sigmoid(gate_pre)
        act = half(gate_pre * sg * up_pre)
        gate_grad = act_grad * up_pre * sg * (1.0 + gate_pre * (1.0 - sg))
        up_grad = act_grad * gate_pre * sg
        both = half(jnp.concatenate([gate_grad, up_grad], axis=1))
        line.end(both)
        acts[part] = Gather(line, act, back_swaps[part])
        grads[part] = Gather(line, both, back_swaps[part])

    rounds = len(bits) - 1

    def both(step, pair):
        for one in pair:
            step(one)

    both(Sum.fold, gu)
    ag[0].fold()
    for _ in range(1, rounds):
        gu[0].fold()
        ag[1].fold()
        gu[1].fold()
        ag[0].fold()
    ag[1].fold()
    both(Sum.finish, gu)
    middle(0)
    middle(1)
    both(Gather.grow, grads)
    for _ in range(1, rounds):
        both(Gather.grow, grads)
        both(Gather.grow, acts)
    both(Gather.grow, acts)

    def back(ids, weights, pairs, jobs, name):
        args = tuple(weights) + tuple(pairs)
        return call(
            functools.partial(back_body, geo, stored, count, jobs),
            [jax.ShapeDtypeStruct((n // 2 * len(jobs), stored), BF16)] * 2,
            (ids,) + args,
            in_specs=[id_spec(total, 0)] + [full(a.shape) for a in args],
            name=name,
        )

    def grad(rows, gathered, at, sources, name):
        cols = slice(at * hidden, (at + 1) * hidden)
        return call(
            functools.partial(grad_body, stored, cols, sources, order),
            jax.ShapeDtypeStruct((count, stored, hidden), BF16),
            (x_rows, rows) + tuple(gathered),
            in_specs=[id_spec(total, 0)] + [full(a.shape) for a in (rows,) + tuple(gathered)],
            grid=(count,),
            out_specs=pl.BlockSpec((1, stored, hidden), lambda e: (e, 0, 0)),
            name=name,
        )

    def joined(mine, other):
        return jnp.concatenate(
            [jnp.where(y == 0, mine, other), jnp.where(y == 0, other, mine)], axis=1
        )

    act_pairs = acts[0].result() + acts[1].result()
    grad_pairs = grads[0].result() + grads[1].result()

    jobs = [(i, ((0, 2 + 2 * i, 0, s), (1, 2 + 2 * i, 1, s))) for i, s in enumerate(sources)]
    keep, send = back(x_rows, (w_gate, w_up), line.begin(*grad_pairs), jobs, "token_rows")
    line.end(send)
    token = Return(line, keep, send)
    (rows,) = line.begin(x_rows)
    grad_gate = line.end(grad(rows, grad_pairs, 0, sources, "grad_gate"))
    jobs = [(i, ((0, 1 + 2 * i, 0, s),)) for i, s in enumerate(sources)]
    keep, send = back(x_rows, (w_down,), line.begin(*act_pairs), jobs, "out_rows")
    line.end(send)
    out = Return(line, keep, send)
    token.fold()
    out.fold()
    for _ in range(1, out.rounds):
        both(Return.fold, (token, out))
    (rows,) = line.begin(x_rows)
    grad_up = line.end(grad(rows, grad_pairs, 1, sources, "grad_up"))
    both(Return.leave, (token, out))
    (rows,) = line.begin(dz_rows)
    grad_down = line.end(grad(rows, act_pairs, 0, sources, "grad_down"))
    token.pieces = line.begin(*token.pieces)
    grad_tokens = joined(*token.pieces)
    out.pieces = line.begin(*out.pieces)
    layer_output = half(f32(joined(*out.pieces)) * route_weights)
    return (layer_output, grad_tokens, grad_gate, grad_up, jnp.swapaxes(grad_down, 1, 2))


def solution(mesh):
    placed = (
        P("ep", "grp"),
        P("ep", None),
        P("ep", None),
        P(),
        P(None, "ep", "grp"),
        P(None, "ep", "grp"),
        P(None, "grp", "ep"),
        P("ep", "grp"),
    )
    return jax.shard_map(
        shards,
        mesh=mesh,
        in_specs=placed,
        out_specs=(
            P("ep", "grp"),
            P("ep", "grp"),
            P(None, "ep", "grp"),
            P(None, "ep", "grp"),
            P(None, "grp", "ep"),
        ),
        check_vma=False,
    )
```

```python
import functools

import jax
import jax.numpy as jnp
from jax import lax
from jax.experimental import pallas as pl
from jax.experimental.pallas import tpu as pltpu
from jax.sharding import PartitionSpec as P

AXES = ("grp", "ep")
BF16 = jnp.bfloat16
VMEM = pl.BlockSpec(memory_space=pltpu.VMEM)
SMEM = pl.BlockSpec(memory_space=pltpu.SMEM)
ROOM = 24
PARTS = 2


def f32(a):
    return a.astype(jnp.float32)


def half(a):
    return a.astype(BF16)


def after(value, *others):
    return lax.optimization_barrier((value,) + others)[0]


def swap(block, grp_bits, ep_bits):
    grp_size, ep_size = lax.axis_size("grp"), lax.axis_size("ep")
    pairs = [
        (g * ep_size + p, (g ^ grp_bits) * ep_size + (p ^ ep_bits))
        for g in range(grp_size)
        for p in range(ep_size)
    ]
    return lax.ppermute(block, AXES, pairs)


def plane_pairs(k):
    grp_size, ep_size = lax.axis_size("grp"), lax.axis_size("ep")
    flip = k * (grp_size // 2)
    return [
        (g * ep_size + p, ((p // 2) ^ flip) * ep_size + 2 * g + ((p % 2) ^ k))
        for g in range(grp_size)
        for p in range(ep_size)
    ]


def column_pairs(across):
    grp_size, ep_size = lax.axis_size("grp"), lax.axis_size("ep")
    top = grp_size // 2
    pairs = []
    for g in range(grp_size):
        for p in range(ep_size):
            z = p // 2
            k = 1 if (g ^ z) & top else 0
            source = g ^ (top if k ^ across else 0)
            target = z ^ (k * top)
            pairs.append((g * ep_size + p, target * ep_size + 2 * source + ((p % 2) ^ k)))
    return pairs


def crossing():
    top = lax.axis_size("grp") // 2
    apart = (lax.axis_index("grp") ^ (lax.axis_index("ep") // 2)) & top
    return (apart != 0).astype(jnp.int32)


class Line:
    def __init__(self):
        self.last = None

    def begin(self, *values):
        if self.last is None:
            return values
        return lax.optimization_barrier(values + (self.last,))[:-1]

    def end(self, value):
        self.last = value
        return value


def summed(terms, rows):
    return functools.reduce(lambda a, b: a + b, [f32(term[rows]) for term in terms])


class Sum:
    def __init__(self, line, keep, send, swaps):
        self.line, self.swaps = line, list(swaps)
        self.terms = [keep]
        self.got = self.swaps.pop(0)(send)

    def fold(self):
        n = self.got.shape[0] // 2
        self.terms[0], self.got = self.line.begin(self.terms[0], self.got)
        terms = self.terms + [self.got]
        send = self.line.end(half(summed(terms, slice(n, None))))
        self.terms = [term[:n] for term in terms]
        self.got = self.swaps.pop(0)(send)

    def finish(self):
        self.terms[0], self.got = self.line.begin(self.terms[0], self.got)
        self.total = self.line.end(summed(self.terms + [self.got], slice(None)))


class Gather:
    def __init__(self, line, own, swaps):
        self.line, self.swaps = line, list(swaps)
        self.held = own
        self.got = self.swaps.pop(0)(own)

    def grow(self):
        held, got = self.line.begin(self.held, self.got)
        self.held = self.line.end(jnp.concatenate([held, got]))
        self.got = self.swaps.pop(0)(self.held)

    def result(self):
        return [self.held, self.got]


class Return:
    def __init__(self, line, keep, send):
        bits = lax.axis_size("grp").bit_length() - 1
        swaps = [functools.partial(swap, grp_bits=1, ep_bits=0)]
        for bit in range(bits - 1, 0, -1):
            swaps.append(functools.partial(swap, grp_bits=1 << bit, ep_bits=0))
        self.rounds = bits - 1
        self.line = line
        self.sum = Sum(line, keep, send, swaps)

    def fold(self):
        self.sum.fold()

    def leave(self):
        total = self.sum
        total.terms[0], total.got = self.line.begin(total.terms[0], total.got)
        n = total.got.shape[0] // 2
        self.pieces = []
        for k in range(2):
            back = [(b, a) for a, b in plane_pairs(k)]
            piece = half(summed(total.terms + [total.got], slice(k * n, (k + 1) * n)))
            self.line.end(piece)
            self.pieces.append(lax.ppermute(piece, AXES, back))


def block_order(bits):
    order = [0]
    for bit in reversed(bits):
        order = order + [j ^ (1 << bit) for j in order]
    return order


def upright(row):
    n = row.shape[1]
    at = lax.broadcasted_iota(jnp.int32, (n, n), 0) == lax.broadcasted_iota(jnp.int32, (n, n), 1)
    return jnp.sum(jnp.where(at, row, jnp.zeros((), row.dtype)), axis=1, keepdims=True)


def cut_body(stored, count, hot_ref, routes_ref, tokens_ref, own_ref, other_ref):
    y = (lax.axis_index("ep") % 2) ^ crossing()
    slot = upright(routes_ref[...])
    expert = slot
    for r in range(hot_ref.shape[0]):
        expert = jnp.where(slot == count + r, hot_ref[r], expert)
    lane = lax.broadcasted_iota(jnp.int32, (slot.shape[0], own_ref.shape[1] - stored), 1)
    tail = half(jnp.where(lane == 0, f32(expert), 0.0))
    rows = tokens_ref[...]
    first, second = rows[:, :stored], rows[:, stored:]
    own_ref[:, :stored] = jnp.where(y == 0, first, second)
    own_ref[:, stored:] = tail
    other_ref[:, :stored] = jnp.where(y == 0, second, first)
    other_ref[:, stored:] = tail


def weigh_body(stored, weights_ref, rows_ref, own_ref, other_ref):
    y = (lax.axis_index("ep") % 2) ^ crossing()
    rows = half(f32(rows_ref[...]) * upright(weights_ref[...]))
    tail = jnp.zeros((rows.shape[0], own_ref.shape[1] - stored), BF16)
    first, second = rows[:, :stored], rows[:, stored:]
    own_ref[:, :stored] = jnp.where(y == 0, first, second)
    own_ref[:, stored:] = tail
    other_ref[:, :stored] = jnp.where(y == 0, second, first)
    other_ref[:, stored:] = tail


def join_body(mine_ref, other_ref, *refs):
    out_ref = refs[-1]
    y = lax.axis_index("ep") % 2
    mine, other = mine_ref[...], other_ref[...]
    n = mine.shape[1]
    halves = jnp.where(y == 0, mine, other), jnp.where(y == 0, other, mine)
    if len(refs) > 1:
        weight = upright(refs[0][...])
        halves = [half(f32(a) * weight) for a in halves]
    out_ref[:, :n] = halves[0]
    out_ref[:, n:] = halves[1]


def order_rows(geo, held_ref, got_ref, rows_ref):
    grp_size, tok, order = geo
    sub = tok // PARTS
    bits = grp_size.bit_length() - 1
    shift = lax.axis_index("grp") ^ (lax.axis_index("ep") // 2)
    for place, j in enumerate(order):
        k = j & 1
        m = shift ^ ((j >> 1) ^ (k * (grp_size // 2)))
        at = 0
        for b in range(bits - 1):
            at = at + (((m >> (bits - 1 - b)) & 1) << b)
        landed = 1 if (j >> 1) & (grp_size // 2) else 0
        src = pl.ds(pl.multiple_of((at * 2 + landed) * tok, tok), tok)
        rows = jnp.where((m & 1) == 0, held_ref[src, :], got_ref[src, :])
        for part in range(PARTS):
            to = (part * len(order) + place) * sub
            rows_ref[to : to + sub, :] = rows[part * sub : (part + 1) * sub]


def expert_dot(rows, expert, w_ref, count, turned):
    zero = jnp.zeros((), BF16)
    own = jnp.concatenate([jnp.where(expert == e, rows, zero) for e in range(count)], axis=1)
    if turned:
        weights = jnp.concatenate([w_ref[e] for e in range(count)], axis=1)
    else:
        weights = w_ref[...].reshape(own.shape[1], w_ref.shape[2])
    dims = (((1,), (1 if turned else 0,)), ((), ()))
    return lax.dot_general(own, weights, dims, preferred_element_type=jnp.float32)


def id_of(id_ref, stored, rows):
    return id_ref[rows, :][:, stored % 128 : stored % 128 + 1]


def first_body(geo, stored, count, n_w, own_ids, part, places, held_ref, got_ref, *refs):
    rows_ref = refs[-1]
    order_rows(geo, held_ref, got_ref, rows_ref)
    n = rows_ref.shape[0] // PARTS
    at = slice(part * n, (part + 1) * n)
    rows = rows_ref[at, :]
    if own_ids:
        expert = rows[:, stored : stored + 1]
        refs = refs[:-1]
    else:
        expert = id_of(refs[0], stored, at)
        refs = refs[1:-1]
    products(rows[:, :stored], expert, count, n_w, refs, places)


def products(rows, expert, count, n_w, refs, places=None):
    n = rows.shape[0] // 2
    places = places or (0, 1)
    size = rows.shape[0] // len(places)
    for i in range(n_w):
        keep_ref, send_ref = refs[n_w + 2 * i : n_w + 2 * i + 2]
        result = half(expert_dot(rows, expert, refs[i], count, False))
        for block, place in enumerate(places):
            out_ref, at = (keep_ref, place * size) if place * size < n else (send_ref, place * size - n)
            out_ref[at : at + size, :] = result[block * size : (block + 1) * size]


def later_body(stored, count, n_w, places, id_ref, rows_ref, *refs):
    expert = id_of(id_ref, stored, slice(None))
    products(rows_ref[:, :stored], expert, count, n_w, refs, places)


def in_order(held, got, source, order):
    n = len(source) // 2
    sub = held.shape[0] // n
    if source == order:
        return [held, got]
    blocks = []
    for j in order:
        place = source.index(j)
        half_of = held if place < n else got
        blocks.append(half_of[(place % n) * sub : (place % n + 1) * sub])
    return [jnp.concatenate(blocks[:n]), jnp.concatenate(blocks[n:])]


def back_body(geo, stored, count, jobs, id_ref, *refs):
    grp_size, tok, order = geo
    keep_ref, send_ref = refs[-2:]
    sub = tok // PARTS
    shift = lax.axis_index("grp") ^ (lax.axis_index("ep") // 2)
    n = len(order) // 2
    for number, (part, terms) in enumerate(jobs):
        for side in range(2):
            at = (part * 2 + side) * n * sub
            expert = id_of(id_ref, stored, slice(at, at + n * sub))
            total = None
            for weight, pair, source in terms:
                rows = in_order(refs[pair][...], refs[pair + 1][...], source, order)[side]
                now = expert_dot(rows, expert, refs[weight], count, True)
                total = now if total is None else total + now
            total = half(total)
            for place in range(n):
                j = order[side * n + place]
                k = j & 1
                m = shift ^ ((j >> 1) ^ (k * (grp_size // 2)))
                to = (((m >> 1) * 2 + k) * len(jobs) + number) * sub
                to = pl.ds(pl.multiple_of(to, sub), sub)
                block = total[place * sub : (place + 1) * sub]

                @pl.when((m & 1) == 0)
                def _():
                    keep_ref[to, :] = block

                @pl.when((m & 1) == 1)
                def _():
                    send_ref[to, :] = block


def grad_body(stored, sources, order, id_ref, rows_ref, *refs):
    out_ref = refs[-1]
    expert = half(pl.program_id(0).astype(jnp.float32))
    right = []
    for part, source in enumerate(sources):
        right += in_order(refs[2 * part][...], refs[2 * part + 1][...], source, order)
    right = jnp.concatenate(right)
    right = jnp.where(id_of(id_ref, stored, slice(None)) == expert, right, jnp.zeros((), BF16))
    out_ref[0] = half(
        lax.dot_general(
            rows_ref[:, :stored],
            right,
            (((0,), (0,)), ((), ())),
            preferred_element_type=jnp.float32,
        )
    )


def full(shape):
    return pl.BlockSpec(shape, lambda *_: (0,) * len(shape))


def shards(tokens, routes, route_weights, hot_experts, w_gate, w_up, w_down, cotangent):
    grp_size, ep_size = lax.axis_size("grp"), lax.axis_size("ep")
    y = lax.axis_index("ep") % 2
    tok = tokens.shape[0]
    w_down = jnp.swapaxes(w_down, 1, 2)
    count, stored, hidden = w_gate.shape
    total = tok * ep_size
    n = total // PARTS
    width = (stored // 128 + 1) * 128
    bits = list(range(ep_size.bit_length() - 1))
    order = block_order(bits)
    geo = (grp_size, tok, order)
    piece = [jax.ShapeDtypeStruct((tok, width), BF16)] * 2

    def call(body, out_shape, args, in_specs=None, name=None, **kw):
        return pl.pallas_call(
            body,
            out_shape=out_shape,
            grid=kw.get("grid", (1,)),
            in_specs=in_specs or [full(a.shape) for a in args],
            out_specs=kw.get("out_specs") or jax.tree.map(lambda o: full(o.shape), out_shape),
            compiler_params=pltpu.CompilerParams(vmem_limit_bytes=kw.get("room", ROOM) << 20),
            cost_estimate=pl.CostEstimate(flops=1, bytes_accessed=1, transcendentals=0),
            name=name,
        )(*args)

    x_pieces = call(
        functools.partial(cut_body, stored, count),
        piece,
        (hot_experts, routes.reshape(1, tok), tokens),
        in_specs=[SMEM, full((1, tok)), full(tokens.shape)],
        name="token_pieces",
        room=60,
    )
    line = Line()
    bit_swaps = [functools.partial(swap, grp_bits=0, ep_bits=1 << bit) for bit in bits]
    grp_bits = range(grp_size.bit_length() - 2, 0, -1)

    apart = crossing()

    def hop(pieces):
        return pieces[0], swap(pieces[1], grp_size // 2, 0)

    def land(pieces):
        stay, got = line.begin(*pieces)
        far = jnp.where(apart == 0, got, stay)
        near = line.end(jnp.where(apart == 0, stay, got))
        far = lax.ppermute(far, AXES, column_pairs(1))
        return [lax.ppermute(near, AXES, column_pairs(0)), far]

    def joined_up(pieces):
        return line.end(jnp.concatenate(line.begin(*pieces)))

    dz_pieces = call(
        functools.partial(weigh_body, stored),
        piece,
        (route_weights.reshape(1, tok), cotangent),
        name="cotangent_pieces",
        room=60,
    )
    x_pieces, dz_pieces = hop(x_pieces), hop(dz_pieces)
    x_landed = land(x_pieces)
    dz_landed = land(dz_pieces)
    x_held, dz_held = joined_up(x_landed), None

    def widened(held):
        return [swap(held, 1 << bit, 0) for bit in grp_bits[:1]]

    def doubled(held, got):
        for i, bit in enumerate(grp_bits):
            held = joined_up((held, got[0] if i == 0 else swap(held, 1 << bit, 0)))
        return held

    x_next = widened(x_held)
    dz_held = joined_up(dz_landed)
    dz_next = widened(dz_held)
    x_held = doubled(x_held, x_next)
    x_got = swap(x_held, 1, 0)

    rows_shape = jax.ShapeDtypeStruct((total, width), BF16)

    def id_spec(rows, at):
        return pl.BlockSpec((rows, 128), lambda *_: (at, stored // 128))

    def split(n_w):
        return [jax.ShapeDtypeStruct((n // 2, hidden), BF16)] * (2 * n_w)

    def later(part, rows, weights, name, places=None):
        return call(
            functools.partial(later_body, stored, count, len(weights), places),
            split(len(weights)),
            (x_rows, rows) + weights,
            in_specs=[
                id_spec(n, part),
                pl.BlockSpec((n, width), lambda *_: (part, 0)),
            ]
            + [full(w.shape) for w in weights],
            name=name,
        )

    turned_bits = [bits[1], bits[0]] + bits[2:]
    turned_order = block_order(turned_bits)
    turned_swaps = [bit_swaps[1], bit_swaps[0]] + bit_swaps[2:]
    places = [turned_order.index(j) for j in order]
    x_held, x_got = line.begin(x_held, x_got)
    keep_g, send_g, keep_u, send_u, x_rows = call(
        functools.partial(first_body, geo, stored, count, 2, True, 1, places),
        split(2) + [rows_shape],
        (x_held, x_got, w_gate, w_up),
        name="gate_up_first",
    )
    line.end(send_g)
    gate_1 = Sum(line, keep_g, send_g, turned_swaps)
    up_1 = Sum(line, keep_u, send_u, turned_swaps)
    (rows,) = line.begin(x_rows)
    keep_g, send_g, keep_u, send_u = later(0, rows, (w_gate, w_up), "gate_up_later")
    line.end(send_g)
    gate_0 = Sum(line, keep_g, send_g, bit_swaps)
    up_0 = Sum(line, keep_u, send_u, bit_swaps)
    dz_held = doubled(dz_held, dz_next)
    dz_got = swap(dz_held, 1, 0)
    gate_1.fold()
    dz_held, dz_got = line.begin(dz_held, dz_got)
    keep, send, dz_rows = call(
        functools.partial(first_body, geo, stored, count, 1, False, 1, places),
        split(1) + [rows_shape],
        (dz_held, dz_got, x_rows, w_down),
        in_specs=[full(dz_held.shape), full(dz_got.shape), id_spec(total, 0), full(w_down.shape)],
        name="act_grad_first",
    )
    line.end(send)
    ag_1 = Sum(line, keep, send, turned_swaps)
    (rows,) = line.begin(dz_rows)
    ag_keep, ag_send = later(0, rows, (w_down,), "act_grad_later")
    line.end(ag_send)

    rounds = len(bits) - 1

    def rest(one):
        for _ in range(1, rounds):
            one.fold()

    gate_0.fold()
    up_1.fold()
    ag_0 = Sum(line, ag_keep, *line.begin(ag_send), bit_swaps)
    up_0.fold()
    rest(gate_1)
    ag_1.fold()
    rest(gate_0)
    rest(up_1)
    gate_1.finish()
    ag_0.fold()
    rest(up_0)
    gate_0.finish()
    rest(ag_1)
    up_1.finish()
    rest(ag_0)
    up_0.finish()
    gate, up, ag = (gate_0, gate_1), (up_0, up_1), (ag_0, ag_1)
    acts, gate_grads, up_grads = [None] * PARTS, [None] * PARTS, [None] * PARTS
    sources = [order, turned_order]
    back_swaps = [bit_swaps[::-1], turned_swaps[::-1]]

    def start_act(part):
        gate_pre, up_pre = gate[part].total, up[part].total
        act = line.end(half(gate_pre * jax.nn.sigmoid(gate_pre) * up_pre))
        acts[part] = Gather(line, act, back_swaps[part])

    def start_grads(part):
        gate_pre, up_pre, act_grad = gate[part].total, up[part].total, ag[part].total
        sg = jax.nn.sigmoid(gate_pre)
        gate_grad = half(act_grad * up_pre * sg * (1.0 + gate_pre * (1.0 - sg)))
        up_grad = half(act_grad * gate_pre * sg)
        line.end(gate_grad)
        gate_grads[part] = Gather(line, gate_grad, back_swaps[part])
        up_grads[part] = Gather(line, up_grad, back_swaps[part])

    start_act(1)
    start_act(0)
    ag_1.finish()
    start_grads(1)
    ag_0.finish()
    start_grads(0)

    def grow(pair):
        pair[1].grow()
        pair[0].grow()

    grow(acts)
    grow(gate_grads)
    for _ in range(1, rounds):
        grow(acts)
    grow(up_grads)
    for _ in range(1, rounds):
        grow(gate_grads)

    def back(ids, weights, pairs, jobs, name):
        args = tuple(weights) + tuple(pairs)
        return call(
            functools.partial(back_body, geo, stored, count, jobs),
            [jax.ShapeDtypeStruct((n // 2 * len(jobs), stored), BF16)] * 2,
            (ids,) + args,
            in_specs=[id_spec(total, 0)] + [full(a.shape) for a in args],
            name=name,
        )

    def grad(rows, gathered, name):
        return call(
            functools.partial(grad_body, stored, sources, order),
            jax.ShapeDtypeStruct((count, stored, hidden), BF16),
            (x_rows, rows) + tuple(gathered),
            in_specs=[id_spec(total, 0)] + [full(a.shape) for a in (rows,) + tuple(gathered)],
            grid=(count,),
            out_specs=pl.BlockSpec((1, stored, hidden), lambda e: (e, 0, 0)),
            name=name,
        )

    def joined(pieces, weights, name):
        args = tuple(pieces) + weights
        return call(join_body, jax.ShapeDtypeStruct(tokens.shape, BF16), args, name=name)

    act_pairs = acts[0].result() + acts[1].result()
    jobs = [(i, ((0, 1 + 2 * i, s),)) for i, s in enumerate(sources)]
    keep, send = back(x_rows, (w_down,), line.begin(*act_pairs), jobs, "out_rows")
    line.end(send)
    out = Return(line, keep, send)
    for _ in range(1, rounds):
        grow(up_grads)
    gate_pairs = gate_grads[0].result() + gate_grads[1].result()
    gate_pairs = line.begin(*gate_pairs)
    grad_gate = line.end(grad(x_rows, gate_pairs, "grad_gate"))
    for _ in range(out.rounds):
        out.fold()
    up_pairs = up_grads[0].result() + up_grads[1].result()
    pairs = line.begin(*up_pairs)
    jobs = [(i, ((0, 2 + 2 * i, s), (1, 6 + 2 * i, s))) for i, s in enumerate(sources)]
    keep, send = back(x_rows, (w_gate, w_up), gate_pairs + pairs, jobs, "token_rows")
    line.end(send)
    token = Return(line, keep, send)
    for _ in range(token.rounds):
        token.fold()
    out.leave()
    (rows,) = line.begin(dz_rows)
    grad_down = line.end(grad(rows, act_pairs, "grad_down"))
    token.leave()
    (rows,) = line.begin(x_rows)
    grad_up = line.end(grad(rows, pairs, "grad_up"))
    weights = (route_weights.reshape(1, tok),)
    layer_output = line.end(joined(line.begin(*out.pieces), weights, "join_output"))
    grad_tokens = line.end(joined(line.begin(*token.pieces), (), "join_tokens"))
    return (layer_output, grad_tokens, grad_gate, grad_up, jnp.swapaxes(grad_down, 1, 2))


def solution(mesh):
    placed = (
        P("ep", "grp"),
        P("ep", None),
        P("ep", None),
        P(),
        P(None, "ep", "grp"),
        P(None, "ep", "grp"),
        P(None, "grp", "ep"),
        P("ep", "grp"),
    )
    return jax.shard_map(
        shards,
        mesh=mesh,
        in_specs=placed,
        out_specs=(
            P("ep", "grp"),
            P("ep", "grp"),
            P(None, "ep", "grp"),
            P(None, "ep", "grp"),
            P(None, "grp", "ep"),
        ),
        check_vma=False,
    )
```

```python
import functools

import jax
import jax.numpy as jnp
from jax import lax
from jax.experimental import pallas as pl
from jax.experimental.pallas import tpu as pltpu
from jax.sharding import PartitionSpec as P

AXES = ("grp", "ep")
BF16 = jnp.bfloat16
VMEM = pl.BlockSpec(memory_space=pltpu.VMEM)
SMEM = pl.BlockSpec(memory_space=pltpu.SMEM)
ROOM = 24
PARTS = 2


def f32(a):
    return a.astype(jnp.float32)


def half(a):
    return a.astype(BF16)


def after(value, *others):
    return lax.optimization_barrier((value,) + others)[0]


def swap(block, grp_bits, ep_bits):
    grp_size, ep_size = lax.axis_size("grp"), lax.axis_size("ep")
    pairs = [
        (g * ep_size + p, (g ^ grp_bits) * ep_size + (p ^ ep_bits))
        for g in range(grp_size)
        for p in range(ep_size)
    ]
    return lax.ppermute(block, AXES, pairs)


def plane_pairs(k):
    grp_size, ep_size = lax.axis_size("grp"), lax.axis_size("ep")
    flip = k * (grp_size // 2)
    return [
        (g * ep_size + p, ((p // 2) ^ flip) * ep_size + 2 * g + ((p % 2) ^ k))
        for g in range(grp_size)
        for p in range(ep_size)
    ]


def column_pairs(across):
    grp_size, ep_size = lax.axis_size("grp"), lax.axis_size("ep")
    top = grp_size // 2
    pairs = []
    for g in range(grp_size):
        for p in range(ep_size):
            z = p // 2
            k = 1 if (g ^ z) & top else 0
            source = g ^ (top if k ^ across else 0)
            target = z ^ (k * top)
            pairs.append((g * ep_size + p, target * ep_size + 2 * source + ((p % 2) ^ k)))
    return pairs


def crossing():
    top = lax.axis_size("grp") // 2
    apart = (lax.axis_index("grp") ^ (lax.axis_index("ep") // 2)) & top
    return (apart != 0).astype(jnp.int32)


class Line:
    def __init__(self):
        self.last = None

    def begin(self, *values):
        if self.last is None:
            return values
        return lax.optimization_barrier(values + (self.last,))[:-1]

    def end(self, value):
        self.last = value
        return value


def summed(terms, rows):
    return functools.reduce(lambda a, b: a + b, [f32(term[rows]) for term in terms])


class Sum:
    def __init__(self, line, keep, send, swaps):
        self.line, self.swaps = line, list(swaps)
        self.terms = [keep]
        self.got = self.swaps.pop(0)(send)

    def fold(self):
        n = self.got.shape[0] // 2
        self.terms[0], self.got = self.line.begin(self.terms[0], self.got)
        terms = self.terms + [self.got]
        send = self.line.end(half(summed(terms, slice(n, None))))
        self.terms = [term[:n] for term in terms]
        self.got = self.swaps.pop(0)(send)

    def finish(self):
        self.terms[0], self.got = self.line.begin(self.terms[0], self.got)
        self.total = self.line.end(summed(self.terms + [self.got], slice(None)))


class Gather:
    def __init__(self, line, own, swaps):
        self.line, self.swaps = line, list(swaps)
        self.held = own
        self.got = self.swaps.pop(0)(own)

    def grow(self):
        held, got = self.line.begin(self.held, self.got)
        self.held = self.line.end(jnp.concatenate([held, got]))
        self.got = self.swaps.pop(0)(self.held)

    def result(self):
        return [self.held, self.got]


class Return:
    def __init__(self, line, keep, send):
        bits = lax.axis_size("grp").bit_length() - 1
        swaps = [functools.partial(swap, grp_bits=1, ep_bits=0)]
        for bit in range(bits - 1, 0, -1):
            swaps.append(functools.partial(swap, grp_bits=1 << bit, ep_bits=0))
        self.rounds = bits - 1
        self.line = line
        self.sum = Sum(line, keep, send, swaps)

    def fold(self):
        self.sum.fold()

    def leave(self):
        total = self.sum
        total.terms[0], total.got = self.line.begin(total.terms[0], total.got)
        n = total.got.shape[0] // 2
        self.pieces = [None, None]
        for k in (1, 0):
            back = [(b, a) for a, b in plane_pairs(k)]
            piece = half(summed(total.terms + [total.got], slice(k * n, (k + 1) * n)))
            self.line.end(piece)
            self.pieces[k] = lax.ppermute(piece, AXES, back)


def block_order(bits):
    order = [0]
    for bit in reversed(bits):
        order = order + [j ^ (1 << bit) for j in order]
    return order


def upright(row):
    n = row.shape[1]
    at = lax.broadcasted_iota(jnp.int32, (n, n), 0) == lax.broadcasted_iota(jnp.int32, (n, n), 1)
    return jnp.sum(jnp.where(at, row, jnp.zeros((), row.dtype)), axis=1, keepdims=True)


def cut_body(stored, count, hot_ref, routes_ref, tokens_ref, own_ref, other_ref):
    y = (lax.axis_index("ep") % 2) ^ crossing()
    slot = upright(routes_ref[...])
    expert = slot
    for r in range(hot_ref.shape[0]):
        expert = jnp.where(slot == count + r, hot_ref[r], expert)
    lane = lax.broadcasted_iota(jnp.int32, (slot.shape[0], own_ref.shape[1] - stored), 1)
    tail = half(jnp.where(lane == 0, f32(expert), 0.0))
    rows = tokens_ref[...]
    first, second = rows[:, :stored], rows[:, stored:]
    own_ref[:, :stored] = jnp.where(y == 0, first, second)
    own_ref[:, stored:] = tail
    other_ref[:, :stored] = jnp.where(y == 0, second, first)
    other_ref[:, stored:] = tail


def weigh_body(stored, weights_ref, rows_ref, own_ref, other_ref):
    y = (lax.axis_index("ep") % 2) ^ crossing()
    rows = half(f32(rows_ref[...]) * upright(weights_ref[...]))
    tail = jnp.zeros((rows.shape[0], own_ref.shape[1] - stored), BF16)
    first, second = rows[:, :stored], rows[:, stored:]
    own_ref[:, :stored] = jnp.where(y == 0, first, second)
    own_ref[:, stored:] = tail
    other_ref[:, :stored] = jnp.where(y == 0, second, first)
    other_ref[:, stored:] = tail


def join_body(mine_ref, other_ref, *refs):
    out_ref = refs[-1]
    y = lax.axis_index("ep") % 2
    mine, other = mine_ref[...], other_ref[...]
    n = mine.shape[1]
    halves = jnp.where(y == 0, mine, other), jnp.where(y == 0, other, mine)
    if len(refs) > 1:
        weight = upright(refs[0][...])
        halves = [half(f32(a) * weight) for a in halves]
    out_ref[:, :n] = halves[0]
    out_ref[:, n:] = halves[1]


def order_rows(geo, held_ref, got_ref, rows_ref):
    grp_size, tok, order = geo
    sub = tok // PARTS
    bits = grp_size.bit_length() - 1
    shift = lax.axis_index("grp") ^ (lax.axis_index("ep") // 2)
    for place, j in enumerate(order):
        k = j & 1
        m = shift ^ ((j >> 1) ^ (k * (grp_size // 2)))
        at = 0
        for b in range(bits - 1):
            at = at + (((m >> (bits - 1 - b)) & 1) << b)
        landed = 1 if (j >> 1) & (grp_size // 2) else 0
        src = pl.ds(pl.multiple_of((at * 2 + landed) * tok, tok), tok)
        rows = jnp.where((m & 1) == 0, held_ref[src, :], got_ref[src, :])
        for part in range(PARTS):
            to = (part * len(order) + place) * sub
            rows_ref[to : to + sub, :] = rows[part * sub : (part + 1) * sub]


def expert_dot(rows, expert, w_ref, count, turned):
    zero = jnp.zeros((), BF16)
    own = jnp.concatenate([jnp.where(expert == e, rows, zero) for e in range(count)], axis=1)
    if turned:
        weights = jnp.concatenate([w_ref[e] for e in range(count)], axis=1)
    else:
        weights = w_ref[...].reshape(own.shape[1], w_ref.shape[2])
    dims = (((1,), (1 if turned else 0,)), ((), ()))
    return lax.dot_general(own, weights, dims, preferred_element_type=jnp.float32)


def id_of(id_ref, stored, rows):
    return id_ref[rows, :][:, stored % 128 : stored % 128 + 1]


def first_body(geo, stored, count, n_w, own_ids, part, places, held_ref, got_ref, *refs):
    rows_ref = refs[-1]
    order_rows(geo, held_ref, got_ref, rows_ref)
    n = rows_ref.shape[0] // PARTS
    at = slice(part * n, (part + 1) * n)
    rows = rows_ref[at, :]
    if own_ids:
        expert = rows[:, stored : stored + 1]
        refs = refs[:-1]
    else:
        expert = id_of(refs[0], stored, at)
        refs = refs[1:-1]
    products(rows[:, :stored], expert, count, n_w, refs, places)


def products(rows, expert, count, n_w, refs, places=None):
    n = rows.shape[0] // 2
    places = places or (0, 1)
    size = rows.shape[0] // len(places)
    for i in range(n_w):
        keep_ref, send_ref = refs[n_w + 2 * i : n_w + 2 * i + 2]
        result = half(expert_dot(rows, expert, refs[i], count, False))
        for block, place in enumerate(places):
            out_ref, at = (keep_ref, place * size) if place * size < n else (send_ref, place * size - n)
            out_ref[at : at + size, :] = result[block * size : (block + 1) * size]


def later_body(stored, count, n_w, places, id_ref, rows_ref, *refs):
    expert = id_of(id_ref, stored, slice(None))
    products(rows_ref[:, :stored], expert, count, n_w, refs, places)


def in_order(held, got, source, order):
    n = len(source) // 2
    sub = held.shape[0] // n
    if source == order:
        return [held, got]
    blocks = []
    for j in order:
        place = source.index(j)
        half_of = held if place < n else got
        blocks.append(half_of[(place % n) * sub : (place % n + 1) * sub])
    return [jnp.concatenate(blocks[:n]), jnp.concatenate(blocks[n:])]


def turned_body(geo, stored, count, sources, id_ref, w_ref, *refs):
    tok, order = geo
    out_ref = refs[-1]
    n = len(order) // 2 * (tok // PARTS)
    for part, source in enumerate(sources):
        pair = in_order(refs[2 * part][...], refs[2 * part + 1][...], source, order)
        for side in range(2):
            at = slice((part * 2 + side) * n, (part * 2 + side + 1) * n)
            out_ref[at, :] = expert_dot(pair[side], id_of(id_ref, stored, at), w_ref, count, True)


def back_body(geo, stored, count, sources, based, id_ref, w_ref, *refs):
    grp_size, tok, order = geo
    keep_ref, send_ref = refs[-2:]
    sub = tok // PARTS
    shift = lax.axis_index("grp") ^ (lax.axis_index("ep") // 2)
    n = len(order) // 2
    for part, source in enumerate(sources):
        pair = in_order(refs[2 * part][...], refs[2 * part + 1][...], source, order)
        for side in range(2):
            at = slice((part * 2 + side) * n * sub, (part * 2 + side + 1) * n * sub)
            total = expert_dot(pair[side], id_of(id_ref, stored, at), w_ref, count, True)
            if based:
                total = total + refs[-3][at, :]
            total = half(total)
            for place in range(n):
                j = order[side * n + place]
                k = j & 1
                m = shift ^ ((j >> 1) ^ (k * (grp_size // 2)))
                to = (((m >> 1) * 2 + k) * len(sources) + part) * sub
                to = pl.ds(pl.multiple_of(to, sub), sub)
                block = total[place * sub : (place + 1) * sub]

                @pl.when((m & 1) == 0)
                def _():
                    keep_ref[to, :] = block

                @pl.when((m & 1) == 1)
                def _():
                    send_ref[to, :] = block


def grad_body(stored, sources, order, id_ref, rows_ref, *refs):
    out_ref = refs[-1]
    expert = half(pl.program_id(0).astype(jnp.float32))
    right = []
    for part, source in enumerate(sources):
        right += in_order(refs[2 * part][...], refs[2 * part + 1][...], source, order)
    right = jnp.concatenate(right)
    right = jnp.where(id_of(id_ref, stored, slice(None)) == expert, right, jnp.zeros((), BF16))
    out_ref[0] = half(
        lax.dot_general(
            rows_ref[:, :stored],
            right,
            (((0,), (0,)), ((), ())),
            preferred_element_type=jnp.float32,
        )
    )


def full(shape):
    return pl.BlockSpec(shape, lambda *_: (0,) * len(shape))


def shards(tokens, routes, route_weights, hot_experts, w_gate, w_up, w_down, cotangent):
    grp_size, ep_size = lax.axis_size("grp"), lax.axis_size("ep")
    y = lax.axis_index("ep") % 2
    tok = tokens.shape[0]
    w_down = jnp.swapaxes(w_down, 1, 2)
    count, stored, hidden = w_gate.shape
    total = tok * ep_size
    n = total // PARTS
    width = (stored // 128 + 1) * 128
    bits = list(range(ep_size.bit_length() - 1))
    order = block_order(bits)
    geo = (grp_size, tok, order)
    piece = [jax.ShapeDtypeStruct((tok, width), BF16)] * 2

    def call(body, out_shape, args, in_specs=None, name=None, **kw):
        return pl.pallas_call(
            body,
            out_shape=out_shape,
            grid=kw.get("grid", (1,)),
            in_specs=in_specs or [full(a.shape) for a in args],
            out_specs=kw.get("out_specs") or jax.tree.map(lambda o: full(o.shape), out_shape),
            compiler_params=pltpu.CompilerParams(vmem_limit_bytes=kw.get("room", ROOM) << 20),
            cost_estimate=pl.CostEstimate(flops=1, bytes_accessed=1, transcendentals=0),
            name=name,
        )(*args)

    x_pieces = call(
        functools.partial(cut_body, stored, count),
        piece,
        (hot_experts, routes.reshape(1, tok), tokens),
        in_specs=[SMEM, full((1, tok)), full(tokens.shape)],
        name="token_pieces",
        room=60,
    )
    line = Line()
    bit_swaps = [functools.partial(swap, grp_bits=0, ep_bits=1 << bit) for bit in bits]
    grp_bits = range(grp_size.bit_length() - 2, 0, -1)

    apart = crossing()

    def hop(pieces):
        return pieces[0], swap(pieces[1], grp_size // 2, 0)

    def land(pieces):
        stay, got = line.begin(*pieces)
        far = jnp.where(apart == 0, got, stay)
        near = line.end(jnp.where(apart == 0, stay, got))
        far = lax.ppermute(far, AXES, column_pairs(1))
        return [lax.ppermute(near, AXES, column_pairs(0)), far]

    def joined_up(pieces):
        return line.end(jnp.concatenate(line.begin(*pieces)))

    dz_pieces = call(
        functools.partial(weigh_body, stored),
        piece,
        (route_weights.reshape(1, tok), cotangent),
        name="cotangent_pieces",
        room=60,
    )
    x_pieces, dz_pieces = hop(x_pieces), hop(dz_pieces)
    x_landed = land(x_pieces)
    dz_landed = land(dz_pieces)
    x_held, dz_held = joined_up(x_landed), None

    def widened(held):
        return [swap(held, 1 << bit, 0) for bit in grp_bits[:1]]

    def doubled(held, got):
        for i, bit in enumerate(grp_bits):
            held = joined_up((held, got[0] if i == 0 else swap(held, 1 << bit, 0)))
        return held

    x_next = widened(x_held)
    dz_held = joined_up(dz_landed)
    dz_next = widened(dz_held)
    x_held = doubled(x_held, x_next)
    x_got = swap(x_held, 1, 0)

    rows_shape = jax.ShapeDtypeStruct((total, width), BF16)

    def id_spec(rows, at):
        return pl.BlockSpec((rows, 128), lambda *_: (at, stored // 128))

    def split(n_w):
        return [jax.ShapeDtypeStruct((n // 2, hidden), BF16)] * (2 * n_w)

    def later(part, rows, weights, name, places=None):
        return call(
            functools.partial(later_body, stored, count, len(weights), places),
            split(len(weights)),
            (x_rows, rows) + weights,
            in_specs=[
                id_spec(n, part),
                pl.BlockSpec((n, width), lambda *_: (part, 0)),
            ]
            + [full(w.shape) for w in weights],
            name=name,
        )

    turned_bits = [bits[1], bits[0]] + bits[2:]
    turned_order = block_order(turned_bits)
    turned_swaps = [bit_swaps[1], bit_swaps[0]] + bit_swaps[2:]
    places = [turned_order.index(j) for j in order]
    x_held, x_got = line.begin(x_held, x_got)
    keep_g, send_g, keep_u, send_u, x_rows = call(
        functools.partial(first_body, geo, stored, count, 2, True, 1, places),
        split(2) + [rows_shape],
        (x_held, x_got, w_gate, w_up),
        name="gate_up_first",
    )
    line.end(send_g)
    gate_1 = Sum(line, keep_g, send_g, turned_swaps)
    up_1 = Sum(line, keep_u, send_u, turned_swaps)
    (rows,) = line.begin(x_rows)
    keep_g, send_g, keep_u, send_u = later(0, rows, (w_gate, w_up), "gate_up_later")
    line.end(send_g)
    gate_0 = Sum(line, keep_g, send_g, bit_swaps)
    up_0 = Sum(line, keep_u, send_u, bit_swaps)
    dz_held = doubled(dz_held, dz_next)
    dz_got = swap(dz_held, 1, 0)
    dz_held, dz_got = line.begin(dz_held, dz_got)
    keep, send, dz_rows = call(
        functools.partial(first_body, geo, stored, count, 1, False, 1, places),
        split(1) + [rows_shape],
        (dz_held, dz_got, x_rows, w_down),
        in_specs=[full(dz_held.shape), full(dz_got.shape), id_spec(total, 0), full(w_down.shape)],
        name="act_grad_first",
    )
    line.end(send)
    ag_1 = Sum(line, keep, send, turned_swaps)
    (rows,) = line.begin(dz_rows)
    ag_keep, ag_send = later(0, rows, (w_down,), "act_grad_later")
    line.end(ag_send)

    rounds = len(bits) - 1

    def rest(one):
        for _ in range(1, rounds):
            one.fold()

    gate_1.fold()
    ag_0 = Sum(line, ag_keep, *line.begin(ag_send), bit_swaps)
    gate_0.fold()
    up_1.fold()
    up_0.fold()
    rest(gate_1)
    ag_1.fold()
    rest(gate_0)
    ag_0.fold()
    rest(up_1)
    gate_1.finish()
    rest(up_0)
    gate_0.finish()
    rest(ag_1)
    rest(ag_0)
    up_1.finish()
    up_0.finish()
    gate, up, ag = (gate_0, gate_1), (up_0, up_1), (ag_0, ag_1)
    acts, gate_grads, up_grads = [None] * PARTS, [None] * PARTS, [None] * PARTS
    pre_grads = [None] * PARTS
    sources = [order, turned_order]
    back_swaps = [bit_swaps[::-1], turned_swaps[::-1]]

    def start_act(part):
        gate_pre, up_pre = gate[part].total, up[part].total
        act = line.end(half(gate_pre * jax.nn.sigmoid(gate_pre) * up_pre))
        acts[part] = Gather(line, act, back_swaps[part])

    def start_grads(part):
        gate_pre, up_pre, act_grad = gate[part].total, up[part].total, ag[part].total
        sg = jax.nn.sigmoid(gate_pre)
        gate_grad = half(act_grad * up_pre * sg * (1.0 + gate_pre * (1.0 - sg)))
        up_grad = half(act_grad * gate_pre * sg)
        line.end(gate_grad)
        gate_grads[part] = Gather(line, gate_grad, back_swaps[part])
        pre_grads[part] = gate_grad, up_grad

    start_act(1)
    start_act(0)
    ag_1.finish()
    start_grads(1)
    ag_0.finish()
    start_grads(0)

    def grow(pair):
        pair[1].grow()
        pair[0].grow()

    grow(acts)
    for part in (1, 0):
        (up_grad,) = line.begin(pre_grads[part][1])
        up_grads[part] = Gather(line, up_grad, back_swaps[part])
    grow(gate_grads)
    for _ in range(1, rounds):
        grow(acts)
    grow(up_grads)
    for _ in range(1, rounds):
        grow(gate_grads)

    def back(weight, pairs, name, base=()):
        args = (weight,) + tuple(pairs) + base
        return call(
            functools.partial(back_body, geo, stored, count, sources, bool(base)),
            [jax.ShapeDtypeStruct((total // 2, stored), BF16)] * 2,
            (x_rows,) + args,
            in_specs=[id_spec(total, 0)] + [full(a.shape) for a in args],
            name=name,
        )

    def grad(rows, gathered, name):
        return call(
            functools.partial(grad_body, stored, sources, order),
            jax.ShapeDtypeStruct((count, stored, hidden), BF16),
            (x_rows, rows) + tuple(gathered),
            in_specs=[id_spec(total, 0)] + [full(a.shape) for a in (rows,) + tuple(gathered)],
            grid=(count,),
            out_specs=pl.BlockSpec((1, stored, hidden), lambda e: (e, 0, 0)),
            name=name,
        )

    def joined(pieces, weights, name):
        args = tuple(pieces) + weights
        return call(join_body, jax.ShapeDtypeStruct(tokens.shape, BF16), args, name=name)

    act_pairs = acts[0].result() + acts[1].result()
    keep, send = back(w_down, line.begin(*act_pairs), "out_rows")
    line.end(send)
    out = Return(line, keep, send)
    for _ in range(1, rounds):
        grow(up_grads)
    for _ in range(out.rounds):
        out.fold()
    gate_pairs = gate_grads[0].result() + gate_grads[1].result()
    gate_pairs = line.begin(*gate_pairs)
    args = (w_gate,) + tuple(gate_pairs)
    base = line.end(
        call(
            functools.partial(turned_body, geo[1:], stored, count, sources),
            jax.ShapeDtypeStruct((total, stored), jnp.float32),
            (x_rows,) + args,
            in_specs=[id_spec(total, 0)] + [full(a.shape) for a in args],
            name="token_gate_rows",
        )
    )
    (rows,) = line.begin(x_rows)
    grad_gate = line.end(grad(rows, gate_pairs, "grad_gate"))
    up_pairs = up_grads[0].result() + up_grads[1].result()
    pairs = line.begin(*up_pairs)
    keep, send = back(w_up, pairs, "token_rows", (base,))
    line.end(send)
    token = Return(line, keep, send)
    out.leave()
    for _ in range(token.rounds):
        token.fold()
    (rows,) = line.begin(dz_rows)
    grad_down = line.end(grad(rows, act_pairs, "grad_down"))
    token.leave()
    (rows,) = line.begin(x_rows)
    grad_up = line.end(grad(rows, pairs, "grad_up"))
    weights = (route_weights.reshape(1, tok),)
    layer_output = line.end(joined(line.begin(*out.pieces), weights, "join_output"))
    grad_tokens = line.end(joined(line.begin(*token.pieces), (), "join_tokens"))
    return (layer_output, grad_tokens, grad_gate, grad_up, jnp.swapaxes(grad_down, 1, 2))


def solution(mesh):
    placed = (
        P("ep", "grp"),
        P("ep", None),
        P("ep", None),
        P(),
        P(None, "ep", "grp"),
        P(None, "ep", "grp"),
        P(None, "grp", "ep"),
        P("ep", "grp"),
    )
    return jax.shard_map(
        shards,
        mesh=mesh,
        in_specs=placed,
        out_specs=(
            P("ep", "grp"),
            P("ep", "grp"),
            P(None, "ep", "grp"),
            P(None, "ep", "grp"),
            P(None, "grp", "ep"),
        ),
        check_vma=False,
    )
```

```python
import functools

import jax
import jax.numpy as jnp
from jax import lax
from jax.experimental import pallas as pl
from jax.experimental.pallas import tpu as pltpu
from jax.sharding import PartitionSpec as P

AXES = ("grp", "ep")
BF16 = jnp.bfloat16
VMEM = pl.BlockSpec(memory_space=pltpu.VMEM)
SMEM = pl.BlockSpec(memory_space=pltpu.SMEM)
ROOM = 24
PARTS = 2


def f32(a):
    return a.astype(jnp.float32)


def half(a):
    return a.astype(BF16)


def after(value, *others):
    return lax.optimization_barrier((value,) + others)[0]


def swap(block, grp_bits, ep_bits):
    grp_size, ep_size = lax.axis_size("grp"), lax.axis_size("ep")
    pairs = [
        (g * ep_size + p, (g ^ grp_bits) * ep_size + (p ^ ep_bits))
        for g in range(grp_size)
        for p in range(ep_size)
    ]
    return lax.ppermute(block, AXES, pairs)


def plane_pairs(k):
    grp_size, ep_size = lax.axis_size("grp"), lax.axis_size("ep")
    flip = k * (grp_size // 2)
    return [
        (g * ep_size + p, ((p // 2) ^ flip) * ep_size + 2 * g + ((p % 2) ^ k))
        for g in range(grp_size)
        for p in range(ep_size)
    ]


def column_pairs(across):
    grp_size, ep_size = lax.axis_size("grp"), lax.axis_size("ep")
    top = grp_size // 2
    pairs = []
    for g in range(grp_size):
        for p in range(ep_size):
            z = p // 2
            k = 1 if (g ^ z) & top else 0
            source = g ^ (top if k ^ across else 0)
            target = z ^ (k * top)
            pairs.append((g * ep_size + p, target * ep_size + 2 * source + ((p % 2) ^ k)))
    return pairs


def crossing():
    top = lax.axis_size("grp") // 2
    apart = (lax.axis_index("grp") ^ (lax.axis_index("ep") // 2)) & top
    return (apart != 0).astype(jnp.int32)


class Line:
    def __init__(self):
        self.last = None

    def begin(self, *values):
        if self.last is None:
            return values
        return lax.optimization_barrier(values + (self.last,))[:-1]

    def end(self, value):
        self.last = value
        return value


def summed(terms, rows):
    return functools.reduce(lambda a, b: a + b, [f32(term[rows]) for term in terms])


class Sum:
    def __init__(self, line, keep, send, swaps):
        self.line, self.swaps = line, list(swaps)
        self.terms = [keep]
        self.got = self.swaps.pop(0)(send)

    def fold(self):
        n = self.got.shape[0] // 2
        self.terms[0], self.got = self.line.begin(self.terms[0], self.got)
        terms = self.terms + [self.got]
        send = self.line.end(half(summed(terms, slice(n, None))))
        self.terms = [term[:n] for term in terms]
        self.got = self.swaps.pop(0)(send)

    def finish(self):
        self.terms[0], self.got = self.line.begin(self.terms[0], self.got)
        self.total = self.line.end(summed(self.terms + [self.got], slice(None)))


class Gather:
    def __init__(self, line, own, swaps):
        self.line, self.swaps = line, list(swaps)
        self.held = own
        self.got = self.swaps.pop(0)(own)

    def grow(self):
        held, got = self.line.begin(self.held, self.got)
        self.held = self.line.end(jnp.concatenate([held, got]))
        self.got = self.swaps.pop(0)(self.held)

    def result(self):
        return [self.held, self.got]


class Return:
    def __init__(self, line, keep, send):
        bits = lax.axis_size("grp").bit_length() - 1
        swaps = [functools.partial(swap, grp_bits=1, ep_bits=0)]
        for bit in range(bits - 1, 0, -1):
            swaps.append(functools.partial(swap, grp_bits=1 << bit, ep_bits=0))
        self.rounds = bits - 1
        self.line = line
        self.sum = Sum(line, keep, send, swaps)

    def fold(self):
        self.sum.fold()

    def leave(self):
        total = self.sum
        total.terms[0], total.got = self.line.begin(total.terms[0], total.got)
        n = total.got.shape[0] // 2
        self.pieces = [None, None]
        for k in (1, 0):
            back = [(b, a) for a, b in plane_pairs(k)]
            piece = half(summed(total.terms + [total.got], slice(k * n, (k + 1) * n)))
            self.line.end(piece)
            self.pieces[k] = lax.ppermute(piece, AXES, back)


def block_order(bits):
    order = [0]
    for bit in reversed(bits):
        order = order + [j ^ (1 << bit) for j in order]
    return order


def upright(row):
    n = row.shape[1]
    at = lax.broadcasted_iota(jnp.int32, (n, n), 0) == lax.broadcasted_iota(jnp.int32, (n, n), 1)
    return jnp.sum(jnp.where(at, row, jnp.zeros((), row.dtype)), axis=1, keepdims=True)


def cut_body(stored, count, hot_ref, routes_ref, tokens_ref, own_ref, other_ref):
    y = (lax.axis_index("ep") % 2) ^ crossing()
    slot = upright(routes_ref[...])
    expert = slot
    for r in range(hot_ref.shape[0]):
        expert = jnp.where(slot == count + r, hot_ref[r], expert)
    lane = lax.broadcasted_iota(jnp.int32, (slot.shape[0], own_ref.shape[1] - stored), 1)
    tail = half(jnp.where(lane == 0, f32(expert), 0.0))
    rows = tokens_ref[...]
    first, second = rows[:, :stored], rows[:, stored:]
    own_ref[:, :stored] = jnp.where(y == 0, first, second)
    own_ref[:, stored:] = tail
    other_ref[:, :stored] = jnp.where(y == 0, second, first)
    other_ref[:, stored:] = tail


def weigh_body(stored, weights_ref, rows_ref, own_ref, other_ref):
    y = (lax.axis_index("ep") % 2) ^ crossing()
    rows = half(f32(rows_ref[...]) * upright(weights_ref[...]))
    tail = jnp.zeros((rows.shape[0], own_ref.shape[1] - stored), BF16)
    first, second = rows[:, :stored], rows[:, stored:]
    own_ref[:, :stored] = jnp.where(y == 0, first, second)
    own_ref[:, stored:] = tail
    other_ref[:, :stored] = jnp.where(y == 0, second, first)
    other_ref[:, stored:] = tail


def join_body(mine_ref, other_ref, *refs):
    out_ref = refs[-1]
    y = lax.axis_index("ep") % 2
    mine, other = mine_ref[...], other_ref[...]
    n = mine.shape[1]
    halves = jnp.where(y == 0, mine, other), jnp.where(y == 0, other, mine)
    if len(refs) > 1:
        weight = upright(refs[0][...])
        halves = [half(f32(a) * weight) for a in halves]
    out_ref[:, :n] = halves[0]
    out_ref[:, n:] = halves[1]


def order_rows(geo, held_ref, got_ref, rows_ref):
    grp_size, tok, order = geo
    sub = tok // PARTS
    bits = grp_size.bit_length() - 1
    shift = lax.axis_index("grp") ^ (lax.axis_index("ep") // 2)
    for place, j in enumerate(order):
        k = j & 1
        m = shift ^ ((j >> 1) ^ (k * (grp_size // 2)))
        at = 0
        for b in range(bits - 1):
            at = at + (((m >> (bits - 1 - b)) & 1) << b)
        landed = 1 if (j >> 1) & (grp_size // 2) else 0
        src = pl.ds(pl.multiple_of((at * 2 + landed) * tok, tok), tok)
        rows = jnp.where((m & 1) == 0, held_ref[src, :], got_ref[src, :])
        for part in range(PARTS):
            to = (part * len(order) + place) * sub
            rows_ref[to : to + sub, :] = rows[part * sub : (part + 1) * sub]


def expert_dot(rows, expert, w_ref, count, turned):
    zero = jnp.zeros((), BF16)
    own = jnp.concatenate([jnp.where(expert == e, rows, zero) for e in range(count)], axis=1)
    if turned:
        weights = jnp.concatenate([w_ref[e] for e in range(count)], axis=1)
    else:
        weights = w_ref[...].reshape(own.shape[1], w_ref.shape[2])
    dims = (((1,), (1 if turned else 0,)), ((), ()))
    return lax.dot_general(own, weights, dims, preferred_element_type=jnp.float32)


def id_of(id_ref, stored, rows):
    return id_ref[rows, :][:, stored % 128 : stored % 128 + 1]


def first_body(geo, stored, count, n_w, own_ids, part, places, held_ref, got_ref, *refs):
    rows_ref = refs[-1]
    order_rows(geo, held_ref, got_ref, rows_ref)
    n = rows_ref.shape[0] // PARTS
    at = slice(part * n, (part + 1) * n)
    rows = rows_ref[at, :]
    if own_ids:
        expert = rows[:, stored : stored + 1]
        refs = refs[:-1]
    else:
        expert = id_of(refs[0], stored, at)
        refs = refs[1:-1]
    products(rows[:, :stored], expert, count, n_w, refs, places)


def products(rows, expert, count, n_w, refs, places=None):
    n = rows.shape[0] // 2
    places = places or (0, 1)
    size = rows.shape[0] // len(places)
    for i in range(n_w):
        keep_ref, send_ref = refs[n_w + 2 * i : n_w + 2 * i + 2]
        result = half(expert_dot(rows, expert, refs[i], count, False))
        for block, place in enumerate(places):
            out_ref, at = (keep_ref, place * size) if place * size < n else (send_ref, place * size - n)
            out_ref[at : at + size, :] = result[block * size : (block + 1) * size]


def later_body(stored, count, n_w, places, id_ref, rows_ref, *refs):
    expert = id_of(id_ref, stored, slice(None))
    products(rows_ref[:, :stored], expert, count, n_w, refs, places)


def in_order(held, got, source, order):
    n = len(source) // 2
    sub = held.shape[0] // n
    if source == order:
        return [held, got]
    blocks = []
    for j in order:
        place = source.index(j)
        half_of = held if place < n else got
        blocks.append(half_of[(place % n) * sub : (place % n + 1) * sub])
    return [jnp.concatenate(blocks[:n]), jnp.concatenate(blocks[n:])]


def turned_body(geo, stored, count, sources, id_ref, w_ref, *refs):
    tok, order = geo
    out_ref = refs[-1]
    n = len(order) // 2 * (tok // PARTS)
    for part, source in enumerate(sources):
        pair = in_order(refs[2 * part][...], refs[2 * part + 1][...], source, order)
        for side in range(2):
            at = slice((part * 2 + side) * n, (part * 2 + side + 1) * n)
            out_ref[at, :] = expert_dot(pair[side], id_of(id_ref, stored, at), w_ref, count, True)


def back_body(geo, stored, count, sources, based, id_ref, w_ref, *refs):
    grp_size, tok, order = geo
    keep_ref, send_ref = refs[-2:]
    sub = tok // PARTS
    shift = lax.axis_index("grp") ^ (lax.axis_index("ep") // 2)
    n = len(order) // 2
    for part, source in enumerate(sources):
        pair = in_order(refs[2 * part][...], refs[2 * part + 1][...], source, order)
        for side in range(2):
            at = slice((part * 2 + side) * n * sub, (part * 2 + side + 1) * n * sub)
            total = expert_dot(pair[side], id_of(id_ref, stored, at), w_ref, count, True)
            if based:
                total = total + refs[-3][at, :]
            total = half(total)
            for place in range(n):
                j = order[side * n + place]
                k = j & 1
                m = shift ^ ((j >> 1) ^ (k * (grp_size // 2)))
                to = (((m >> 1) * 2 + k) * len(sources) + part) * sub
                to = pl.ds(pl.multiple_of(to, sub), sub)
                block = total[place * sub : (place + 1) * sub]

                @pl.when((m & 1) == 0)
                def _():
                    keep_ref[to, :] = block

                @pl.when((m & 1) == 1)
                def _():
                    send_ref[to, :] = block


def grad_body(stored, sources, order, id_ref, rows_ref, *refs):
    out_ref = refs[-1]
    expert = half(pl.program_id(0).astype(jnp.float32))
    right = []
    for part, source in enumerate(sources):
        right += in_order(refs[2 * part][...], refs[2 * part + 1][...], source, order)
    right = jnp.concatenate(right)
    right = jnp.where(id_of(id_ref, stored, slice(None)) == expert, right, jnp.zeros((), BF16))
    out_ref[0] = half(
        lax.dot_general(
            rows_ref[:, :stored],
            right,
            (((0,), (0,)), ((), ())),
            preferred_element_type=jnp.float32,
        )
    )


def full(shape):
    return pl.BlockSpec(shape, lambda *_: (0,) * len(shape))


def shards(tokens, routes, route_weights, hot_experts, w_gate, w_up, w_down, cotangent):
    grp_size, ep_size = lax.axis_size("grp"), lax.axis_size("ep")
    y = lax.axis_index("ep") % 2
    tok = tokens.shape[0]
    w_down = jnp.swapaxes(w_down, 1, 2)
    count, stored, hidden = w_gate.shape
    total = tok * ep_size
    n = total // PARTS
    width = (stored // 128 + 1) * 128
    bits = list(range(ep_size.bit_length() - 1))
    order = block_order(bits)
    geo = (grp_size, tok, order)
    piece = [jax.ShapeDtypeStruct((tok, width), BF16)] * 2

    def call(body, out_shape, args, in_specs=None, name=None, **kw):
        return pl.pallas_call(
            body,
            out_shape=out_shape,
            grid=kw.get("grid", (1,)),
            in_specs=in_specs or [full(a.shape) for a in args],
            out_specs=kw.get("out_specs") or jax.tree.map(lambda o: full(o.shape), out_shape),
            compiler_params=pltpu.CompilerParams(vmem_limit_bytes=kw.get("room", ROOM) << 20),
            cost_estimate=pl.CostEstimate(flops=10**9, bytes_accessed=2*10**6, transcendentals=0),
            name=name,
        )(*args)

    x_pieces = call(
        functools.partial(cut_body, stored, count),
        piece,
        (hot_experts, routes.reshape(1, tok), tokens),
        in_specs=[SMEM, full((1, tok)), full(tokens.shape)],
        name="token_pieces",
        room=60,
    )
    line = Line()
    bit_swaps = [functools.partial(swap, grp_bits=0, ep_bits=1 << bit) for bit in bits]
    grp_bits = range(grp_size.bit_length() - 2, 0, -1)

    apart = crossing()

    def hop(pieces):
        return pieces[0], swap(pieces[1], grp_size // 2, 0)

    def land(pieces):
        stay, got = line.begin(*pieces)
        far = jnp.where(apart == 0, got, stay)
        near = line.end(jnp.where(apart == 0, stay, got))
        far = lax.ppermute(far, AXES, column_pairs(1))
        return [lax.ppermute(near, AXES, column_pairs(0)), far]

    def joined_up(pieces):
        return line.end(jnp.concatenate(line.begin(*pieces)))

    dz_pieces = call(
        functools.partial(weigh_body, stored),
        piece,
        (route_weights.reshape(1, tok), cotangent),
        name="cotangent_pieces",
        room=60,
    )
    x_pieces, dz_pieces = hop(x_pieces), hop(dz_pieces)
    x_landed = land(x_pieces)
    dz_landed = land(dz_pieces)
    x_held, dz_held = joined_up(x_landed), None

    def widened(held):
        return [swap(held, 1 << bit, 0) for bit in grp_bits[:1]]

    def doubled(held, got):
        for i, bit in enumerate(grp_bits):
            held = joined_up((held, got[0] if i == 0 else swap(held, 1 << bit, 0)))
        return held

    x_next = widened(x_held)
    dz_held = joined_up(dz_landed)
    dz_next = widened(dz_held)
    x_held = doubled(x_held, x_next)
    x_got = swap(x_held, 1, 0)

    rows_shape = jax.ShapeDtypeStruct((total, width), BF16)

    def id_spec(rows, at):
        return pl.BlockSpec((rows, 128), lambda *_: (at, stored // 128))

    def split(n_w):
        return [jax.ShapeDtypeStruct((n // 2, hidden), BF16)] * (2 * n_w)

    def later(part, rows, weights, name, places=None):
        return call(
            functools.partial(later_body, stored, count, len(weights), places),
            split(len(weights)),
            (x_rows, rows) + weights,
            in_specs=[
                id_spec(n, part),
                pl.BlockSpec((n, width), lambda *_: (part, 0)),
            ]
            + [full(w.shape) for w in weights],
            name=name,
        )

    turned_bits = [bits[1], bits[0]] + bits[2:]
    turned_order = block_order(turned_bits)
    turned_swaps = [bit_swaps[1], bit_swaps[0]] + bit_swaps[2:]
    places = [turned_order.index(j) for j in order]
    x_held, x_got = line.begin(x_held, x_got)
    keep_g, send_g, keep_u, send_u, x_rows = call(
        functools.partial(first_body, geo, stored, count, 2, True, 1, places),
        split(2) + [rows_shape],
        (x_held, x_got, w_gate, w_up),
        name="gate_up_first",
    )
    line.end(send_g)
    gate_1 = Sum(line, keep_g, send_g, turned_swaps)
    up_1 = Sum(line, keep_u, send_u, turned_swaps)
    (rows,) = line.begin(x_rows)
    keep_g, send_g, keep_u, send_u = later(0, rows, (w_gate, w_up), "gate_up_later")
    line.end(send_g)
    gate_0 = Sum(line, keep_g, send_g, bit_swaps)
    up_0 = Sum(line, keep_u, send_u, bit_swaps)
    dz_held = doubled(dz_held, dz_next)
    dz_got = swap(dz_held, 1, 0)
    dz_held, dz_got = line.begin(dz_held, dz_got)
    keep, send, dz_rows = call(
        functools.partial(first_body, geo, stored, count, 1, False, 1, places),
        split(1) + [rows_shape],
        (dz_held, dz_got, x_rows, w_down),
        in_specs=[full(dz_held.shape), full(dz_got.shape), id_spec(total, 0), full(w_down.shape)],
        name="act_grad_first",
    )
    line.end(send)
    ag_1 = Sum(line, keep, send, turned_swaps)
    (rows,) = line.begin(dz_rows)
    ag_keep, ag_send = later(0, rows, (w_down,), "act_grad_later")
    line.end(ag_send)

    rounds = len(bits) - 1

    def rest(one):
        for _ in range(1, rounds):
            one.fold()

    gate_1.fold()
    ag_0 = Sum(line, ag_keep, *line.begin(ag_send), bit_swaps)
    gate_0.fold()
    up_1.fold()
    up_0.fold()
    rest(gate_1)
    ag_1.fold()
    rest(gate_0)
    ag_0.fold()
    rest(up_1)
    gate_1.finish()
    rest(up_0)
    gate_0.finish()
    rest(ag_1)
    rest(ag_0)
    up_1.finish()
    up_0.finish()
    gate, up, ag = (gate_0, gate_1), (up_0, up_1), (ag_0, ag_1)
    acts, gate_grads, up_grads = [None] * PARTS, [None] * PARTS, [None] * PARTS
    pre_grads = [None] * PARTS
    sources = [order, turned_order]
    back_swaps = [bit_swaps[::-1], turned_swaps[::-1]]

    def start_act(part):
        gate_pre, up_pre = gate[part].total, up[part].total
        act = line.end(half(gate_pre * jax.nn.sigmoid(gate_pre) * up_pre))
        acts[part] = Gather(line, act, back_swaps[part])

    def start_grads(part):
        gate_pre, up_pre, act_grad = gate[part].total, up[part].total, ag[part].total
        sg = jax.nn.sigmoid(gate_pre)
        gate_grad = half(act_grad * up_pre * sg * (1.0 + gate_pre * (1.0 - sg)))
        up_grad = half(act_grad * gate_pre * sg)
        line.end(gate_grad)
        gate_grads[part] = Gather(line, gate_grad, back_swaps[part])
        pre_grads[part] = gate_grad, up_grad

    start_act(1)
    start_act(0)
    ag_1.finish()
    start_grads(1)
    ag_0.finish()
    start_grads(0)

    def grow(pair):
        pair[1].grow()
        pair[0].grow()

    grow(acts)
    for part in (1, 0):
        (up_grad,) = line.begin(pre_grads[part][1])
        up_grads[part] = Gather(line, up_grad, back_swaps[part])
    grow(gate_grads)
    for _ in range(1, rounds):
        grow(acts)
    grow(up_grads)
    for _ in range(1, rounds):
        grow(gate_grads)

    def back(weight, pairs, name, base=()):
        args = (weight,) + tuple(pairs) + base
        return call(
            functools.partial(back_body, geo, stored, count, sources, bool(base)),
            [jax.ShapeDtypeStruct((total // 2, stored), BF16)] * 2,
            (x_rows,) + args,
            in_specs=[id_spec(total, 0)] + [full(a.shape) for a in args],
            name=name,
        )

    def grad(rows, gathered, name):
        return call(
            functools.partial(grad_body, stored, sources, order),
            jax.ShapeDtypeStruct((count, stored, hidden), BF16),
            (x_rows, rows) + tuple(gathered),
            in_specs=[id_spec(total, 0)] + [full(a.shape) for a in (rows,) + tuple(gathered)],
            grid=(count,),
            out_specs=pl.BlockSpec((1, stored, hidden), lambda e: (e, 0, 0)),
            name=name,
        )

    def joined(pieces, weights, name):
        args = tuple(pieces) + weights
        return call(join_body, jax.ShapeDtypeStruct(tokens.shape, BF16), args, name=name)

    act_pairs = acts[0].result() + acts[1].result()
    keep, send = back(w_down, line.begin(*act_pairs), "out_rows")
    line.end(send)
    out = Return(line, keep, send)
    for _ in range(1, rounds):
        grow(up_grads)
    for _ in range(out.rounds):
        out.fold()
    gate_pairs = gate_grads[0].result() + gate_grads[1].result()
    gate_pairs = line.begin(*gate_pairs)
    args = (w_gate,) + tuple(gate_pairs)
    base = line.end(
        call(
            functools.partial(turned_body, geo[1:], stored, count, sources),
            jax.ShapeDtypeStruct((total, stored), jnp.float32),
            (x_rows,) + args,
            in_specs=[id_spec(total, 0)] + [full(a.shape) for a in args],
            name="token_gate_rows",
        )
    )
    (rows,) = line.begin(x_rows)
    grad_gate = line.end(grad(rows, gate_pairs, "grad_gate"))
    up_pairs = up_grads[0].result() + up_grads[1].result()
    pairs = line.begin(*up_pairs)
    keep, send = back(w_up, pairs, "token_rows", (base,))
    line.end(send)
    token = Return(line, keep, send)
    out.leave()
    for _ in range(token.rounds):
        token.fold()
    (rows,) = line.begin(dz_rows)
    grad_down = line.end(grad(rows, act_pairs, "grad_down"))
    token.leave()
    (rows,) = line.begin(x_rows)
    grad_up = line.end(grad(rows, pairs, "grad_up"))
    weights = (route_weights.reshape(1, tok),)
    layer_output = line.end(joined(line.begin(*out.pieces), weights, "join_output"))
    grad_tokens = line.end(joined(line.begin(*token.pieces), (), "join_tokens"))
    return (layer_output, grad_tokens, grad_gate, grad_up, jnp.swapaxes(grad_down, 1, 2))


def solution(mesh):
    placed = (
        P("ep", "grp"),
        P("ep", None),
        P("ep", None),
        P(),
        P(None, "ep", "grp"),
        P(None, "ep", "grp"),
        P(None, "grp", "ep"),
        P("ep", "grp"),
    )
    return jax.shard_map(
        shards,
        mesh=mesh,
        in_specs=placed,
        out_specs=(
            P("ep", "grp"),
            P("ep", "grp"),
            P(None, "ep", "grp"),
            P(None, "ep", "grp"),
            P(None, "grp", "ep"),
        ),
        check_vma=False,
    )
```

```python
import functools

import jax
import jax.numpy as jnp
from jax import lax
from jax.experimental import pallas as pl
from jax.experimental.pallas import tpu as pltpu
from jax.sharding import PartitionSpec as P

AXES = ("grp", "ep")
BF16 = jnp.bfloat16
VMEM = pl.BlockSpec(memory_space=pltpu.VMEM)
SMEM = pl.BlockSpec(memory_space=pltpu.SMEM)
ROOM = 24
PARTS = 2


def f32(a):
    return a.astype(jnp.float32)


def half(a):
    return a.astype(BF16)


def after(value, *others):
    return lax.optimization_barrier((value,) + others)[0]


def swap(block, grp_bits, ep_bits):
    grp_size, ep_size = lax.axis_size("grp"), lax.axis_size("ep")
    pairs = [
        (g * ep_size + p, (g ^ grp_bits) * ep_size + (p ^ ep_bits))
        for g in range(grp_size)
        for p in range(ep_size)
    ]
    return lax.ppermute(block, AXES, pairs)


def plane_pairs(k):
    grp_size, ep_size = lax.axis_size("grp"), lax.axis_size("ep")
    flip = k * (grp_size // 2)
    return [
        (g * ep_size + p, ((p // 2) ^ flip) * ep_size + 2 * g + ((p % 2) ^ k))
        for g in range(grp_size)
        for p in range(ep_size)
    ]


def column_pairs(across):
    grp_size, ep_size = lax.axis_size("grp"), lax.axis_size("ep")
    top = grp_size // 2
    pairs = []
    for g in range(grp_size):
        for p in range(ep_size):
            z = p // 2
            k = 1 if (g ^ z) & top else 0
            source = g ^ (top if k ^ across else 0)
            target = z ^ (k * top)
            pairs.append((g * ep_size + p, target * ep_size + 2 * source + ((p % 2) ^ k)))
    return pairs


def crossing():
    top = lax.axis_size("grp") // 2
    apart = (lax.axis_index("grp") ^ (lax.axis_index("ep") // 2)) & top
    return (apart != 0).astype(jnp.int32)


class Line:
    def __init__(self):
        self.last = None

    def begin(self, *values):
        if self.last is None:
            return values
        return lax.optimization_barrier(values + (self.last,))[:-1]

    def end(self, value):
        self.last = value
        return value


def summed(terms, rows):
    return functools.reduce(lambda a, b: a + b, [f32(term[rows]) for term in terms])


class Sum:
    def __init__(self, line, keep, send, swaps):
        self.line, self.swaps = line, list(swaps)
        self.terms = [keep]
        self.got = self.swaps.pop(0)(send)

    def fold(self):
        n = self.got.shape[0] // 2
        self.terms[0], self.got = self.line.begin(self.terms[0], self.got)
        terms = self.terms + [self.got]
        send = self.line.end(half(summed(terms, slice(n, None))))
        self.terms = [term[:n] for term in terms]
        self.got = self.swaps.pop(0)(send)

    def finish(self):
        self.terms[0], self.got = self.line.begin(self.terms[0], self.got)
        self.total = self.line.end(summed(self.terms + [self.got], slice(None)))


class Gather:
    def __init__(self, line, own, swaps):
        self.line, self.swaps = line, list(swaps)
        self.held = own
        self.got = self.swaps.pop(0)(own)

    def grow(self):
        held, got = self.line.begin(self.held, self.got)
        self.held = self.line.end(jnp.concatenate([held, got]))
        self.got = self.swaps.pop(0)(self.held)

    def result(self):
        return [self.held, self.got]


class Return:
    def __init__(self, line, keep, send):
        bits = lax.axis_size("grp").bit_length() - 1
        swaps = [functools.partial(swap, grp_bits=1, ep_bits=0)]
        for bit in range(bits - 1, 0, -1):
            swaps.append(functools.partial(swap, grp_bits=1 << bit, ep_bits=0))
        self.rounds = bits - 1
        self.line = line
        self.sum = Sum(line, keep, send, swaps)

    def fold(self):
        self.sum.fold()

    def leave(self):
        total = self.sum
        total.terms[0], total.got = self.line.begin(total.terms[0], total.got)
        n = total.got.shape[0] // 2
        self.pieces = [None, None]
        for k in (1, 0):
            back = [(b, a) for a, b in plane_pairs(k)]
            piece = half(summed(total.terms + [total.got], slice(k * n, (k + 1) * n)))
            self.line.end(piece)
            self.pieces[k] = lax.ppermute(piece, AXES, back)


def block_order(bits):
    order = [0]
    for bit in reversed(bits):
        order = order + [j ^ (1 << bit) for j in order]
    return order


def upright(row):
    n = row.shape[1]
    at = lax.broadcasted_iota(jnp.int32, (n, n), 0) == lax.broadcasted_iota(jnp.int32, (n, n), 1)
    return jnp.sum(jnp.where(at, row, jnp.zeros((), row.dtype)), axis=1, keepdims=True)


def cut_body(stored, count, hot_ref, routes_ref, tokens_ref, own_ref, other_ref):
    y = (lax.axis_index("ep") % 2) ^ crossing()
    slot = upright(routes_ref[...])
    expert = slot
    for r in range(hot_ref.shape[0]):
        expert = jnp.where(slot == count + r, hot_ref[r], expert)
    lane = lax.broadcasted_iota(jnp.int32, (slot.shape[0], own_ref.shape[1] - stored), 1)
    tail = half(jnp.where(lane == 0, f32(expert), 0.0))
    rows = tokens_ref[...]
    first, second = rows[:, :stored], rows[:, stored:]
    own_ref[:, :stored] = jnp.where(y == 0, first, second)
    own_ref[:, stored:] = tail
    other_ref[:, :stored] = jnp.where(y == 0, second, first)
    other_ref[:, stored:] = tail


def weigh_body(stored, weights_ref, rows_ref, own_ref, other_ref):
    y = (lax.axis_index("ep") % 2) ^ crossing()
    rows = half(f32(rows_ref[...]) * upright(weights_ref[...]))
    tail = jnp.zeros((rows.shape[0], own_ref.shape[1] - stored), BF16)
    first, second = rows[:, :stored], rows[:, stored:]
    own_ref[:, :stored] = jnp.where(y == 0, first, second)
    own_ref[:, stored:] = tail
    other_ref[:, :stored] = jnp.where(y == 0, second, first)
    other_ref[:, stored:] = tail


def join_body(mine_ref, other_ref, *refs):
    out_ref = refs[-1]
    y = lax.axis_index("ep") % 2
    mine, other = mine_ref[...], other_ref[...]
    n = mine.shape[1]
    halves = jnp.where(y == 0, mine, other), jnp.where(y == 0, other, mine)
    if len(refs) > 1:
        weight = upright(refs[0][...])
        halves = [half(f32(a) * weight) for a in halves]
    out_ref[:, :n] = halves[0]
    out_ref[:, n:] = halves[1]


def order_rows(geo, held_ref, got_ref, rows_ref):
    grp_size, tok, order = geo
    sub = tok // PARTS
    bits = grp_size.bit_length() - 1
    shift = lax.axis_index("grp") ^ (lax.axis_index("ep") // 2)
    for place, j in enumerate(order):
        k = j & 1
        m = shift ^ ((j >> 1) ^ (k * (grp_size // 2)))
        at = 0
        for b in range(bits - 1):
            at = at + (((m >> (bits - 1 - b)) & 1) << b)
        landed = 1 if (j >> 1) & (grp_size // 2) else 0
        src = pl.ds(pl.multiple_of((at * 2 + landed) * tok, tok), tok)
        rows = jnp.where((m & 1) == 0, held_ref[src, :], got_ref[src, :])
        for part in range(PARTS):
            to = (part * len(order) + place) * sub
            rows_ref[to : to + sub, :] = rows[part * sub : (part + 1) * sub]


def expert_dot(rows, expert, w_ref, count, turned):
    zero = jnp.zeros((), BF16)
    own = jnp.concatenate([jnp.where(expert == e, rows, zero) for e in range(count)], axis=1)
    if turned:
        weights = jnp.concatenate([w_ref[e] for e in range(count)], axis=1)
    else:
        weights = w_ref[...].reshape(own.shape[1], w_ref.shape[2])
    dims = (((1,), (1 if turned else 0,)), ((), ()))
    return lax.dot_general(own, weights, dims, preferred_element_type=jnp.float32)


def id_of(id_ref, stored, rows):
    return id_ref[rows, :][:, stored % 128 : stored % 128 + 1]


def first_body(geo, stored, count, n_w, own_ids, part, places, held_ref, got_ref, *refs):
    rows_ref = refs[-1]
    order_rows(geo, held_ref, got_ref, rows_ref)
    n = rows_ref.shape[0] // PARTS
    at = slice(part * n, (part + 1) * n)
    rows = rows_ref[at, :]
    if own_ids:
        expert = rows[:, stored : stored + 1]
        refs = refs[:-1]
    else:
        expert = id_of(refs[0], stored, at)
        refs = refs[1:-1]
    products(rows[:, :stored], expert, count, n_w, refs, places)


def products(rows, expert, count, n_w, refs, places=None):
    n = rows.shape[0] // 2
    places = places or (0, 1)
    size = rows.shape[0] // len(places)
    for i in range(n_w):
        keep_ref, send_ref = refs[n_w + 2 * i : n_w + 2 * i + 2]
        result = half(expert_dot(rows, expert, refs[i], count, False))
        for block, place in enumerate(places):
            out_ref, at = (keep_ref, place * size) if place * size < n else (send_ref, place * size - n)
            out_ref[at : at + size, :] = result[block * size : (block + 1) * size]


def later_body(stored, count, n_w, places, id_ref, rows_ref, *refs):
    expert = id_of(id_ref, stored, slice(None))
    products(rows_ref[:, :stored], expert, count, n_w, refs, places)


def in_order(held, got, source, order):
    n = len(source) // 2
    sub = held.shape[0] // n
    if source == order:
        return [held, got]
    blocks = []
    for j in order:
        place = source.index(j)
        half_of = held if place < n else got
        blocks.append(half_of[(place % n) * sub : (place % n + 1) * sub])
    return [jnp.concatenate(blocks[:n]), jnp.concatenate(blocks[n:])]


def turned_body(geo, stored, count, sources, id_ref, w_ref, *refs):
    tok, order = geo
    out_ref = refs[-1]
    n = len(order) // 2 * (tok // PARTS)
    for part, source in enumerate(sources):
        pair = in_order(refs[2 * part][...], refs[2 * part + 1][...], source, order)
        for side in range(2):
            at = slice((part * 2 + side) * n, (part * 2 + side + 1) * n)
            out_ref[at, :] = expert_dot(pair[side], id_of(id_ref, stored, at), w_ref, count, True)


def back_body(geo, stored, count, sources, based, id_ref, w_ref, *refs):
    grp_size, tok, order = geo
    keep_ref, send_ref = refs[-2:]
    sub = tok // PARTS
    shift = lax.axis_index("grp") ^ (lax.axis_index("ep") // 2)
    n = len(order) // 2
    for part, source in enumerate(sources):
        pair = in_order(refs[2 * part][...], refs[2 * part + 1][...], source, order)
        for side in range(2):
            at = slice((part * 2 + side) * n * sub, (part * 2 + side + 1) * n * sub)
            total = expert_dot(pair[side], id_of(id_ref, stored, at), w_ref, count, True)
            if based:
                total = total + refs[-3][at, :]
            total = half(total)
            for place in range(n):
                j = order[side * n + place]
                k = j & 1
                m = shift ^ ((j >> 1) ^ (k * (grp_size // 2)))
                to = (((m >> 1) * 2 + k) * len(sources) + part) * sub
                to = pl.ds(pl.multiple_of(to, sub), sub)
                block = total[place * sub : (place + 1) * sub]

                @pl.when((m & 1) == 0)
                def _():
                    keep_ref[to, :] = block

                @pl.when((m & 1) == 1)
                def _():
                    send_ref[to, :] = block


def grad_body(stored, sources, order, id_ref, rows_ref, *refs):
    out_ref = refs[-1]
    expert = half(pl.program_id(0).astype(jnp.float32))
    right = []
    for part, source in enumerate(sources):
        right += in_order(refs[2 * part][...], refs[2 * part + 1][...], source, order)
    right = jnp.concatenate(right)
    right = jnp.where(id_of(id_ref, stored, slice(None)) == expert, right, jnp.zeros((), BF16))
    out_ref[0] = half(
        lax.dot_general(
            rows_ref[:, :stored],
            right,
            (((0,), (0,)), ((), ())),
            preferred_element_type=jnp.float32,
        )
    )


def full(shape):
    return pl.BlockSpec(shape, lambda *_: (0,) * len(shape))


def shards(tokens, routes, route_weights, hot_experts, w_gate, w_up, w_down, cotangent):
    grp_size, ep_size = lax.axis_size("grp"), lax.axis_size("ep")
    y = lax.axis_index("ep") % 2
    tok = tokens.shape[0]
    w_down = jnp.swapaxes(w_down, 1, 2)
    count, stored, hidden = w_gate.shape
    total = tok * ep_size
    n = total // PARTS
    width = (stored // 128 + 1) * 128
    bits = list(range(ep_size.bit_length() - 1))
    order = block_order(bits)
    geo = (grp_size, tok, order)
    piece = [jax.ShapeDtypeStruct((tok, width), BF16)] * 2

    def call(body, out_shape, args, in_specs=None, name=None, **kw):
        return pl.pallas_call(
            body,
            out_shape=out_shape,
            grid=kw.get("grid", (1,)),
            in_specs=in_specs or [full(a.shape) for a in args],
            out_specs=kw.get("out_specs") or jax.tree.map(lambda o: full(o.shape), out_shape),
            compiler_params=pltpu.CompilerParams(vmem_limit_bytes=kw.get("room", ROOM) << 20),
            cost_estimate=pl.CostEstimate(flops=10**9, bytes_accessed=2*10**6, transcendentals=0),
            name=name,
        )(*args)

    x_pieces = call(
        functools.partial(cut_body, stored, count),
        piece,
        (hot_experts, routes.reshape(1, tok), tokens),
        in_specs=[SMEM, full((1, tok)), full(tokens.shape)],
        name="token_pieces",
        room=60,
    )
    line = Line()
    bit_swaps = [functools.partial(swap, grp_bits=0, ep_bits=1 << bit) for bit in bits]
    grp_bits = range(grp_size.bit_length() - 2, 0, -1)

    apart = crossing()

    def hop(pieces):
        return pieces[0], swap(pieces[1], grp_size // 2, 0)

    def land(pieces):
        stay, got = line.begin(*pieces)
        far = jnp.where(apart == 0, got, stay)
        near = line.end(jnp.where(apart == 0, stay, got))
        far = lax.ppermute(far, AXES, column_pairs(1))
        return [lax.ppermute(near, AXES, column_pairs(0)), far]

    def joined_up(pieces):
        return line.end(jnp.concatenate(line.begin(*pieces)))

    dz_pieces = call(
        functools.partial(weigh_body, stored),
        piece,
        (route_weights.reshape(1, tok), cotangent),
        name="cotangent_pieces",
        room=60,
    )
    x_pieces, dz_pieces = hop(x_pieces), hop(dz_pieces)
    x_landed = land(x_pieces)
    dz_landed = land(dz_pieces)
    x_held, dz_held = joined_up(x_landed), None

    def widened(held):
        return [swap(held, 1 << bit, 0) for bit in grp_bits[:1]]

    def doubled(held, got):
        for i, bit in enumerate(grp_bits):
            held = joined_up((held, got[0] if i == 0 else swap(held, 1 << bit, 0)))
        return held

    x_next = widened(x_held)
    dz_held = joined_up(dz_landed)
    dz_next = widened(dz_held)
    x_held = doubled(x_held, x_next)
    x_got = swap(x_held, 1, 0)

    rows_shape = jax.ShapeDtypeStruct((total, width), BF16)

    def id_spec(rows, at):
        return pl.BlockSpec((rows, 128), lambda *_: (at, stored // 128))

    def split(n_w):
        return [jax.ShapeDtypeStruct((n // 2, hidden), BF16)] * (2 * n_w)

    def later(part, rows, weights, name, places=None):
        return call(
            functools.partial(later_body, stored, count, len(weights), places),
            split(len(weights)),
            (x_rows, rows) + weights,
            in_specs=[
                id_spec(n, part),
                pl.BlockSpec((n, width), lambda *_: (part, 0)),
            ]
            + [full(w.shape) for w in weights],
            name=name,
        )

    turned_bits = [bits[1], bits[0]] + bits[2:]
    turned_order = block_order(turned_bits)
    turned_swaps = [bit_swaps[1], bit_swaps[0]] + bit_swaps[2:]
    places = [turned_order.index(j) for j in order]
    x_held, x_got = line.begin(x_held, x_got)
    keep_g, send_g, keep_u, send_u, x_rows = call(
        functools.partial(first_body, geo, stored, count, 2, True, 1, places),
        split(2) + [rows_shape],
        (x_held, x_got, w_gate, w_up),
        name="gate_up_first",
    )
    line.end(send_g)
    gate_1 = Sum(line, keep_g, send_g, turned_swaps)
    up_1 = Sum(line, keep_u, send_u, turned_swaps)
    (rows,) = line.begin(x_rows)
    keep_g, send_g, keep_u, send_u = later(0, rows, (w_gate, w_up), "gate_up_later")
    line.end(send_g)
    gate_0 = Sum(line, keep_g, send_g, bit_swaps)
    up_0 = Sum(line, keep_u, send_u, bit_swaps)
    dz_held = doubled(dz_held, dz_next)
    dz_got = swap(dz_held, 1, 0)
    dz_held, dz_got = line.begin(dz_held, dz_got)
    keep, send, dz_rows = call(
        functools.partial(first_body, geo, stored, count, 1, False, 1, places),
        split(1) + [rows_shape],
        (dz_held, dz_got, x_rows, w_down),
        in_specs=[full(dz_held.shape), full(dz_got.shape), id_spec(total, 0), full(w_down.shape)],
        name="act_grad_first",
    )
    line.end(send)
    ag_1 = Sum(line, keep, send, turned_swaps)
    (rows,) = line.begin(dz_rows)
    ag_keep, ag_send = later(0, rows, (w_down,), "act_grad_later")
    line.end(ag_send)

    rounds = len(bits) - 1

    def rest(one):
        for _ in range(1, rounds):
            one.fold()

    gate_1.fold()
    ag_0 = Sum(line, ag_keep, *line.begin(ag_send), bit_swaps)
    gate_0.fold()
    up_1.fold()
    up_0.fold()
    rest(gate_1)
    ag_1.fold()
    rest(gate_0)
    ag_0.fold()
    rest(up_1)
    gate_1.finish()
    rest(up_0)
    gate_0.finish()
    rest(ag_1)
    rest(ag_0)
    up_1.finish()
    up_0.finish()
    gate, up, ag = (gate_0, gate_1), (up_0, up_1), (ag_0, ag_1)
    acts, gate_grads, up_grads = [None] * PARTS, [None] * PARTS, [None] * PARTS
    pre_grads = [None] * PARTS
    sources = [order, turned_order]
    back_swaps = [bit_swaps[::-1], turned_swaps[::-1]]

    def start_act(part):
        gate_pre, up_pre = gate[part].total, up[part].total
        act = line.end(half(gate_pre * jax.nn.sigmoid(gate_pre) * up_pre))
        acts[part] = Gather(line, act, back_swaps[part])

    def start_grads(part):
        gate_pre, up_pre, act_grad = gate[part].total, up[part].total, ag[part].total
        sg = jax.nn.sigmoid(gate_pre)
        gate_grad = half(act_grad * up_pre * sg * (1.0 + gate_pre * (1.0 - sg)))
        up_grad = half(act_grad * gate_pre * sg)
        line.end(gate_grad)
        gate_grads[part] = Gather(line, gate_grad, back_swaps[part])
        pre_grads[part] = gate_grad, up_grad

    start_act(1)
    start_act(0)
    ag_1.finish()
    start_grads(1)
    ag_0.finish()
    start_grads(0)

    def grow(pair):
        pair[1].grow()
        pair[0].grow()

    grow(acts)
    for part in (1, 0):
        (up_grad,) = line.begin(pre_grads[part][1])
        up_grads[part] = Gather(line, up_grad, back_swaps[part])
    grow(gate_grads)
    for _ in range(1, rounds):
        grow(acts)
    grow(up_grads)
    for _ in range(1, rounds):
        grow(gate_grads)

    def back(weight, pairs, name, base=()):
        args = (weight,) + tuple(pairs) + base
        return call(
            functools.partial(back_body, geo, stored, count, sources, bool(base)),
            [jax.ShapeDtypeStruct((total // 2, stored), BF16)] * 2,
            (x_rows,) + args,
            in_specs=[id_spec(total, 0)] + [full(a.shape) for a in args],
            name=name,
        )

    def grad(rows, gathered, name):
        return call(
            functools.partial(grad_body, stored, sources, order),
            jax.ShapeDtypeStruct((count, stored, hidden), BF16),
            (x_rows, rows) + tuple(gathered),
            in_specs=[id_spec(total, 0)] + [full(a.shape) for a in (rows,) + tuple(gathered)],
            grid=(count,),
            out_specs=pl.BlockSpec((1, stored, hidden), lambda e: (e, 0, 0)),
            name=name,
        )

    def joined(pieces, weights, name):
        args = tuple(pieces) + weights
        return call(join_body, jax.ShapeDtypeStruct(tokens.shape, BF16), args, name=name)

    act_pairs = acts[0].result() + acts[1].result()
    keep, send = back(w_down, line.begin(*act_pairs), "out_rows")
    line.end(send)
    out = Return(line, keep, send)
    for _ in range(1, rounds):
        grow(up_grads)
    for _ in range(out.rounds):
        out.fold()
    gate_pairs = gate_grads[0].result() + gate_grads[1].result()
    gate_pairs = line.begin(*gate_pairs)
    args = (w_gate,) + tuple(gate_pairs)
    base = line.end(
        call(
            functools.partial(turned_body, geo[1:], stored, count, sources),
            jax.ShapeDtypeStruct((total, stored), jnp.float32),
            (x_rows,) + args,
            in_specs=[id_spec(total, 0)] + [full(a.shape) for a in args],
            name="token_gate_rows",
        )
    )
    (rows,) = line.begin(x_rows)
    grad_gate = line.end(grad(rows, gate_pairs, "grad_gate"))
    up_pairs = up_grads[0].result() + up_grads[1].result()
    pairs = line.begin(*up_pairs)
    keep, send = back(w_up, pairs, "token_rows", (base,))
    line.end(send)
    token = Return(line, keep, send)
    out.leave()
    for _ in range(token.rounds):
        token.fold()
    (rows,) = line.begin(dz_rows)
    grad_down = line.end(grad(rows, act_pairs, "grad_down"))
    token.leave()
    weights = (route_weights.reshape(1, tok),)
    layer_output = line.end(joined(line.begin(*out.pieces), weights, "join_output"))
    (rows,) = line.begin(x_rows)
    grad_up = line.end(grad(rows, pairs, "grad_up"))
    grad_tokens = line.end(joined(line.begin(*token.pieces), (), "join_tokens"))
    return (layer_output, grad_tokens, grad_gate, grad_up, jnp.swapaxes(grad_down, 1, 2))


def solution(mesh):
    placed = (
        P("ep", "grp"),
        P("ep", None),
        P("ep", None),
        P(),
        P(None, "ep", "grp"),
        P(None, "ep", "grp"),
        P(None, "grp", "ep"),
        P("ep", "grp"),
    )
    return jax.shard_map(
        shards,
        mesh=mesh,
        in_specs=placed,
        out_specs=(
            P("ep", "grp"),
            P("ep", "grp"),
            P(None, "ep", "grp"),
            P(None, "ep", "grp"),
            P(None, "grp", "ep"),
        ),
        check_vma=False,
    )
```
